128 devices in a mesh: patch: 32 (over x, y, core), tensor: 2 (over z_lo), guide: 2 (over z_hi).
Axes of the slice: x: 4, y: 4, z: 4 (z_hi: 2, z_lo: 2; z = z_hi * 2 + z_lo), core: 2. Of those that a mesh axis runs over, the one named last changes fastest.
Arguments:
- fresh_q: bfloat16 [2, 6144, 2560], P('guide', 'patch', 'tensor'), may hold values from -61 to 61
- fresh_k: bfloat16 [2, 6144, 2560], P('guide', 'patch', 'tensor'), may hold values from -45 to 45
- fresh_v: bfloat16 [2, 6144, 2560], P('guide', 'patch', 'tensor'), may hold values from -6 to 6
- stale_k: bfloat16 [2, 6144, 2560], P('guide', 'patch', 'tensor'), may hold values from -45 to 45
- stale_v: bfloat16 [2, 6144, 2560], P('guide', 'patch', 'tensor'), may hold values from -6 to 6
- positions: int32 [3, 6144], P(None, 'patch'), may hold values from 0 to 31
- residual: bfloat16 [2, 6144, 5120], P('guide', 'patch', 'tensor'), may hold values from -3 to 3
- out_weight: bfloat16 [2560, 5120], P('tensor'), may hold values from -0.125 to 0.125
- gate_table: float32 [50, 5120], replicated, may hold values from 0.3 to 3
- timestep: int32 [1], replicated, may hold values from 0 to 49
Outputs:
- guided: bfloat16 [6144, 5120], P('patch', ('tensor', 'guide'))
The draws below stay inside these ranges and needn't reach their ends.
All inputs are finite; a program needn't handle non-finite values.
Results may differ from the reference program's by a relative error of at most 0.011.
Values may be sent and summed in bfloat16 or wider, within the bound.
A program may use at most 128 MiB of HBM per device.

```python
import math
import jax
import jax.numpy as jnp
from jax import lax

D = 5120
HEADS = 20
HEAD_DIM = 128
STEPS = 50
GRID = 32
TOK_DEV = 192
TOKENS = 6144
HD = 2560
N_PATCH = 32


def key_entries(key, salt):
    base_key = jax.random.fold_in(key, salt)
    entries = jnp.clip(2.5 * jax.random.normal(base_key, (2, TOKENS, HEADS, HEAD_DIM), jnp.float32), -12.0, 12.0)
    return entries.reshape(2, TOKENS, HEADS * HEAD_DIM)


def draw_fresh_k(key, part):
    return key_entries(key, 17).astype(jnp.bfloat16)


def draw_stale_k(key, part):
    return key_entries(key, 19).astype(jnp.bfloat16)


def draw_fresh_q(key, part):
    base_key = jax.random.fold_in(key, 13)
    entries = jnp.clip(jax.random.normal(base_key, (2, TOKENS, HEADS, HEAD_DIM), jnp.float32), -6.0, 6.0)
    return entries.reshape(2, TOKENS, HEADS * HEAD_DIM).astype(jnp.bfloat16)


def with_ends(values, rng, smallest, top_value):
    dims = values.shape
    spot = [jax.random.randint(jax.random.fold_in(rng, axis), (), 0, dims[axis]) for axis in range(len(dims))]
    values = values.at[tuple(spot)].set(smallest)
    longest = dims.index(max(dims))
    spot[longest] = (spot[longest] + 1) % dims[longest]
    return values.at[tuple(spot)].set(top_value)


def block_levels(own_key, dims, cuts, least, high):
    def one(axis_at, parts):
        heights = jax.random.uniform(jax.random.fold_in(jax.random.fold_in(own_key, 6), axis_at), (parts,), jnp.float32, least / len(cuts), high / len(cuts))
        return jnp.repeat(jnp.exp(heights), dims[axis_at] // parts).reshape((-1,) + (1,) * (len(dims) - axis_at - 1))

    gain = one(*cuts[0])
    for cut in cuts[1:]:
        gain = gain * one(*cut)
    return gain


def bell_draw(own_key, shape, deviation, reach, pieces=(), kind=jnp.bfloat16):
    drawn = jax.random.normal(own_key, shape, jnp.float32) * deviation
    if len(pieces) > 0:
        drawn = block_levels(own_key, shape, pieces, -0.22, 0.18) * drawn
    return jnp.clip(drawn, min=-reach, max=reach).astype(kind)


def setup_inputs(seed: int = 0) -> dict:
    key_list = jax.random.split(jax.random.key(seed), 11)
    return {
        "fresh_q": draw_fresh_q(jax.random.fold_in(key_list[10], 71), 0),
        "fresh_k": draw_fresh_k(jax.random.fold_in(key_list[10], 71), 0),
        "fresh_v": bell_draw(key_list[2], (2, TOKENS, HD), 1.0, 6.0, ((0, 2), (1, 32), (2, 2))),
        "stale_k": draw_stale_k(jax.random.fold_in(key_list[10], 71), 0),
        "stale_v": bell_draw(key_list[4], (2, TOKENS, HD), 1.0, 6.0, ((0, 2), (1, 32), (2, 2))),
        "positions": with_ends(jax.random.randint(key_list[5], (3, TOKENS), 0, GRID), jax.random.fold_in(key_list[5], 1), 0, GRID - 1).astype(jnp.int32),
        "residual": bell_draw(key_list[6], (2, TOKENS, D), 0.5, 3.0, ((0, 2), (1, 32), (2, 2))),
        "out_weight": bell_draw(key_list[7], (HD, D), HD ** -0.5, 0.125, ((0, 2),)),
        "gate_table": jnp.clip(jnp.exp(jax.random.uniform(key_list[8], (STEPS, D), jnp.float32, math.log(0.3), math.log(3.0))), 0.3, 3.0),
        "timestep": jax.random.randint(key_list[9], (1,), 0, STEPS).astype(jnp.int32),
    }


def rotate_positions(values, positions):
    rows_count = values.shape[0]
    width = values.shape[1]
    head_count = width // HEAD_DIM
    half_dim = HEAD_DIM // 2
    side_pairs = HEAD_DIM // 6
    frame_pairs = half_dim - 2 * side_pairs
    pair_index = lax.iota(jnp.int32, half_dim)
    section = (pair_index >= frame_pairs).astype(jnp.int32) + (pair_index >= frame_pairs + side_pairs).astype(jnp.int32)
    local_index = pair_index - jnp.where(section == 0, 0, jnp.where(section == 1, frame_pairs, frame_pairs + side_pairs))
    section_pairs = jnp.where(section == 0, frame_pairs, side_pairs)
    exponent = local_index.astype(jnp.float32) / section_pairs.astype(jnp.float32)
    freqs = jnp.power(jnp.float32(10000.0), -exponent)
    place = positions.astype(jnp.float32)
    chosen = jnp.where(section[None, :] == 0, place[0][:, None], jnp.where(section[None, :] == 1, place[1][:, None], place[2][:, None]))
    angles = chosen * freqs[None, :]
    cosines = jnp.repeat(jnp.cos(angles), 2, axis=1)
    sines = jnp.repeat(jnp.sin(angles), 2, axis=1)
    row_ids = lax.iota(jnp.int32, HEAD_DIM)[:, None]
    col_ids = lax.iota(jnp.int32, HEAD_DIM)[None, :]
    swap_table = jnp.where((row_ids % 2 == 1) & (col_ids == row_ids - 1), -1.0, jnp.where((row_ids % 2 == 0) & (col_ids == row_ids + 1), 1.0, 0.0)).astype(jnp.float32)
    shaped = values.astype(jnp.float32).reshape(rows_count, head_count, HEAD_DIM)
    turned = jnp.einsum('thd,de->the', shaped, swap_table, precision=lax.Precision.HIGHEST)
    result = shaped * cosines[:, None, :] + turned * sines[:, None, :]
    return result.reshape(rows_count, width)

def reference(fresh_q, fresh_k, fresh_v, stale_k, stale_v, positions, residual, out_weight, gate_table, timestep):
    queries = jnp.stack([rotate_positions(fresh_q[0], positions), rotate_positions(fresh_q[1], positions)]).astype(jnp.bfloat16)
    new_keys = jnp.stack([rotate_positions(fresh_k[0], positions), rotate_positions(fresh_k[1], positions)]).astype(jnp.bfloat16)
    queries = lax.optimization_barrier(queries)
    new_keys = lax.optimization_barrier(new_keys)
    score_scale = 1.0 / math.sqrt(HEAD_DIM)

    def attend_block(index):
        branch = index // N_PATCH
        block = index % N_PATCH
        start = (block * TOK_DEV).astype(jnp.int32)
        branch_q = lax.dynamic_index_in_dim(queries, branch, 0, keepdims=False)
        branch_k = lax.dynamic_index_in_dim(new_keys, branch, 0, keepdims=False)
        branch_v = lax.dynamic_index_in_dim(fresh_v, branch, 0, keepdims=False)
        old_k = lax.dynamic_index_in_dim(stale_k, branch, 0, keepdims=False)
        old_v = lax.dynamic_index_in_dim(stale_v, branch, 0, keepdims=False)
        query_rows = lax.dynamic_slice_in_dim(branch_q, start, TOK_DEV, 0)
        key_rows = lax.dynamic_update_slice_in_dim(old_k, lax.dynamic_slice_in_dim(branch_k, start, TOK_DEV, 0), start, 0)
        value_rows = lax.dynamic_update_slice_in_dim(old_v, lax.dynamic_slice_in_dim(branch_v, start, TOK_DEV, 0), start, 0)
        q_heads = query_rows.astype(jnp.float32).reshape(TOK_DEV, HEADS, HEAD_DIM)
        k_heads = key_rows.astype(jnp.float32).reshape(TOKENS, HEADS, HEAD_DIM)
        v_heads = value_rows.astype(jnp.float32).reshape(TOKENS, HEADS, HEAD_DIM)
        scores = jnp.einsum('qhd,khd->hqk', q_heads, k_heads) * score_scale
        top_score = lax.optimization_barrier(jnp.max(scores, axis=2, keepdims=True))
        expo = jnp.exp(scores - top_score)
        total = lax.optimization_barrier(jnp.sum(expo, axis=2))
        weights = lax.optimization_barrier(expo.astype(jnp.bfloat16)).astype(jnp.float32)
        summed = jnp.einsum('hqk,khd->qhd', weights, v_heads)
        result = summed / jnp.transpose(total)[:, :, None]
        return result.reshape(TOK_DEV, HD).astype(jnp.bfloat16)
    blocks = lax.map(attend_block, jnp.arange(2 * N_PATCH, dtype=jnp.int32))
    attn = blocks.reshape(2, TOKENS, HD)
    one_hot = (lax.iota(jnp.int32, STEPS) == timestep[0]).astype(jnp.float32)[None, :]
    gate_row = jnp.dot(one_hot, gate_table, precision=lax.Precision.HIGHEST, preferred_element_type=jnp.float32)
    hidden_cond = residual[0].astype(jnp.float32) + gate_row * jnp.dot(attn[0], out_weight, preferred_element_type=jnp.float32)
    hidden_uncond = residual[1].astype(jnp.float32) + gate_row * jnp.dot(attn[1], out_weight, preferred_element_type=jnp.float32)
    guided = hidden_uncond + 5.0 * (hidden_cond - hidden_uncond)
    return guided.astype(jnp.bfloat16)
```

```python
import functools
import math

import jax
import jax.numpy as jnp
import numpy as np
from jax import lax
from jax.experimental import pallas as pl
from jax.experimental.pallas import tpu as pltpu
from jax.sharding import PartitionSpec as P

MESH = pl.DeviceIdType.MESH
BF = jnp.bfloat16
F32 = jnp.float32
HEAD_DIM = 128
GUIDE_SCALE = 5.0
RING = 4
ROWS = 192
GROUP = 5
HEADS = 10
KEYS = 8 * ROWS
NOTE = 16
HALF = 640
SCORE_SCALE = math.log2(math.e) / math.sqrt(HEAD_DIM)

(K_LEFT, K_RIGHT, V_LEFT, V_RIGHT, K_FAR, V_FAR, Q_LEFT, Q_RIGHT, Q_FAR, SIB_K, SIB_V, SIB_FK, SIB_FV, SIB_Q) = range(14)
KINDS = 14


def frequencies():
    half_dim = HEAD_DIM // 2
    side_pairs = HEAD_DIM // 6
    frame_pairs = half_dim - 2 * side_pairs
    table = np.zeros((8, HEAD_DIM), np.float32)
    for pair in range(half_dim):
        if pair < frame_pairs:
            section, local, size = 0, pair, frame_pairs
        elif pair < frame_pairs + side_pairs:
            section, local, size = 1, pair - frame_pairs, side_pairs
        else:
            section, local, size = 2, pair - frame_pairs - side_pairs, side_pairs
        table[section, 2 * pair : 2 * pair + 2] = 10000.0 ** (-local / size)
    return table


def block_rows(index, count=1):
    return pl.ds(pl.multiple_of(index * ROWS, ROWS), count * ROWS)


def head_columns(head):
    return pl.ds(pl.multiple_of(head * HEAD_DIM, HEAD_DIM), HEAD_DIM)


def same_lane(rows):
    shape = (rows, HEAD_DIM)
    return lax.broadcasted_iota(jnp.int32, shape, 0) == lax.broadcasted_iota(jnp.int32, shape, 1)


def kernel(
    fresh_q, fresh_k, fresh_v, stale_k, stale_v, residual, weight, gate_table, freqs, positions, timestep,
    out,
    kb, vb, qb, q_raw, k_raw, q_rot, k_rot, o_send, o_recv, attn, attn_other, combined, w_tiles, part_send, part_recv,
    part_own, res_own, res_other, gate_rows, cosines, sines,
    recv, o_recv_sem, kv_sem, q_sem, far_sem, sib_sem, local_sem, o_sem, guide_send, guide_recv, part_send_sem,
    part_recv_sem, res_sem, load_sem,
):
    p, t, g = lax.axis_index("patch"), lax.axis_index("tensor"), lax.axis_index("guide")
    x, y, c = p // (2 * RING), (p // 2) % RING, p % 2
    sib = 1 - c

    def at(dx, dy, core):
        return (((x + dx) % RING * RING + (y + dy) % RING) * 2 + core, t, g)

    def send(src, dst, send_sem, recv_sem, device):
        pltpu.make_async_remote_copy(
            src_ref=src, dst_ref=dst, send_sem=send_sem, recv_sem=recv_sem, device_id=device, device_id_type=MESH
        ).start()

    def await_bytes(ref, sem):
        pltpu.make_async_copy(ref, ref, sem).wait()

    def got(kind, i):
        return recv.at[kind * GROUP + i]

    own_slot, fresh_slot = 1 + 7 * c, 9 - 9 * c

    load_q = pltpu.make_async_copy(fresh_q.at[0], q_raw, load_sem.at[0])
    load_k = pltpu.make_async_copy(fresh_k.at[0], k_raw, load_sem.at[1])
    load_q.start()
    load_k.start()

    peers = [at(dx, 0, core) for dx in (1, 3) for core in (0, 1)]
    peers += [at(0, dy, core) for dy in (1, 2, 3) for core in (0, 1)]
    peers += [at(0, 0, sib), (p, 1 - t, g), (p, 1 - t, 1 - g), (p, t, 1 - g)]
    barrier = pltpu.get_barrier_semaphore()
    for peer in peers:
        pl.semaphore_signal(barrier, inc=1, device_id=peer, device_id_type=MESH)

    def local_stale(i, start):
        columns = head_columns(GROUP * c + i)
        copies = (
            pltpu.make_async_copy(stale_k.at[0, :, columns], kb.at[i, block_rows(own_slot), :], local_sem.at[i, 0]),
            pltpu.make_async_copy(stale_v.at[0, :, columns], vb.at[i, block_rows(own_slot), :], local_sem.at[i, 1]),
            pltpu.make_async_copy(fresh_v.at[0, :, columns], vb.at[i, block_rows(fresh_slot), :], local_sem.at[i, 2]),
        )
        for copy in copies:
            copy.start() if start else copy.wait()

    def local_rotated(i, start):
        head = GROUP * c + i
        copies = (
            pltpu.make_async_copy(k_rot.at[head], kb.at[i, block_rows(fresh_slot), :], local_sem.at[i, 3]),
            pltpu.make_async_copy(q_rot.at[head], qb.at[i, block_rows(c), :], local_sem.at[i, 4]),
        )
        for copy in copies:
            copy.start() if start else copy.wait()

    def send_own(i):
        for core in (0, 1):
            columns = head_columns(GROUP * core + i)
            for tensor, (source, buf) in enumerate(((stale_k, kb), (stale_v, vb))):
                for way, (dx, slot, kind) in enumerate(((1, 2, 2 * tensor), (3, 4, 2 * tensor + 1))):
                    send(
                        source.at[0, :, columns],
                        buf.at[i, block_rows(slot + c), :],
                        kv_sem.at[i, core * 4 + tensor * 2 + way],
                        got(kind, i),
                        at(dx, 0, core),
                    )

    def send_sibling_stale(i):
        columns = head_columns(GROUP * sib + i)
        device = at(0, 0, sib)
        send(stale_k.at[0, :, columns], kb.at[i, block_rows(own_slot), :], sib_sem.at[i, 0], got(SIB_K, i), device)
        send(stale_v.at[0, :, columns], vb.at[i, block_rows(own_slot), :], sib_sem.at[i, 1], got(SIB_V, i), device)
        send(fresh_v.at[0, :, columns], vb.at[i, block_rows(fresh_slot), :], sib_sem.at[i, 2], got(SIB_FV, i), device)

    def send_rotated(i):
        head = GROUP * sib + i
        device = at(0, 0, sib)
        send(q_rot.at[head], qb.at[i, block_rows(c), :], sib_sem.at[i, 3], got(SIB_Q, i), device)
        send(k_rot.at[head], kb.at[i, block_rows(fresh_slot), :], sib_sem.at[i, 4], got(SIB_FK, i), device)
        for core in (0, 1):
            for way, (dy, block, kind) in enumerate(((1, 6, Q_LEFT), (3, 2, Q_RIGHT))):
                send(
                    q_rot.at[GROUP * core + i],
                    qb.at[i, block_rows(block + c), :],
                    q_sem.at[i, core * 2 + way],
                    got(kind, i),
                    at(0, dy, core),
                )

    def forward(i):
        await_bytes(kb.at[i, block_rows(2, 2), :], got(K_LEFT, i))
        send(
            kb.at[i, block_rows(2, 2), :], kb.at[i, block_rows(6, 2), :], far_sem.at[i, 0], got(K_FAR, i), at(1, 0, c)
        )
        await_bytes(vb.at[i, block_rows(4, 2), :], got(V_RIGHT, i))
        send(
            vb.at[i, block_rows(4, 2), :], vb.at[i, block_rows(6, 2), :], far_sem.at[i, 1], got(V_FAR, i), at(3, 0, c)
        )
        await_bytes(qb.at[i, block_rows(6, 2), :], got(Q_LEFT, i))
        send(qb.at[i, block_rows(6), :], qb.at[i, block_rows(4), :], far_sem.at[i, 2], got(Q_FAR, i), at(0, 1, c))
        await_bytes(qb.at[i, block_rows(2, 2), :], got(Q_RIGHT, i))
        send(qb.at[i, block_rows(3), :], qb.at[i, block_rows(5), :], far_sem.at[i, 3], got(Q_FAR, i), at(0, 3, c))

    def arrived(i):
        local_stale(i, False)
        local_rotated(i, False)
        other = 8 - 7 * c
        other_fresh = 9 * c
        await_bytes(kb.at[i, block_rows(other), :], got(SIB_K, i))
        await_bytes(vb.at[i, block_rows(other), :], got(SIB_V, i))
        await_bytes(kb.at[i, block_rows(other_fresh), :], got(SIB_FK, i))
        await_bytes(vb.at[i, block_rows(other_fresh), :], got(SIB_FV, i))
        await_bytes(qb.at[i, block_rows(sib), :], got(SIB_Q, i))
        await_bytes(kb.at[i, block_rows(4, 2), :], got(K_RIGHT, i))
        await_bytes(vb.at[i, block_rows(2, 2), :], got(V_LEFT, i))
        await_bytes(kb.at[i, block_rows(6, 2), :], got(K_FAR, i))
        await_bytes(vb.at[i, block_rows(6, 2), :], got(V_FAR, i))
        await_bytes(qb.at[i, block_rows(4, 2), :], got(Q_FAR, i))

    pl.semaphore_wait(barrier, len(peers))
    send_own(0)

    @pl.loop(0, GROUP)
    def _(i):
        local_stale(i, True)
        send_sibling_stale(i)

    res_columns = residual.shape[2] // 2
    mine = pl.ds(pl.multiple_of(g * res_columns, HEAD_DIM), res_columns)
    partner = pl.ds(pl.multiple_of((1 - g) * res_columns, HEAD_DIM), res_columns)

    where_at = positions[...].astype(F32)
    row_of = lax.broadcasted_iota(jnp.int32, (8, ROWS), 0)
    places = jnp.where(
        row_of == 0, where_at[0:1], jnp.where(row_of == 1, where_at[1:2], jnp.where(row_of == 2, where_at[2:3], 0.0))
    )
    angles = lax.dot_general(
        places, freqs[...], (((0,), (0,)), ((), ())), precision=lax.Precision.HIGHEST, preferred_element_type=F32
    )
    cosines[...] = jnp.cos(angles)
    sines[...] = jnp.sin(angles)
    row_ids = lax.broadcasted_iota(jnp.int32, (HEAD_DIM, HEAD_DIM), 0)
    col_ids = lax.broadcasted_iota(jnp.int32, (HEAD_DIM, HEAD_DIM), 1)
    swap = jnp.where(
        (row_ids % 2 == 1) & (col_ids == row_ids - 1),
        -1.0,
        jnp.where((row_ids % 2 == 0) & (col_ids == row_ids + 1), 1.0, 0.0),
    ).astype(BF)

    def rotated(raw, head):
        values = raw[:, head_columns(head)]
        turned = jnp.dot(values, swap, preferred_element_type=F32)
        return (values.astype(F32) * cosines[...] + turned * sines[...]).astype(BF)

    load_q.wait()
    load_k.wait()

    @pl.loop(0, GROUP)
    def _(i):
        for core in (0, 1):
            head = GROUP * core + i
            q_rot[head] = rotated(q_raw, head)
            k_rot[head] = rotated(k_raw, head)
        send_rotated(i)
        local_rotated(i, True)

    send_own(1)

    send(residual.at[0, :, partner], res_other, res_sem.at[0], res_sem.at[1], (p, t, 1 - g))
    width = 2 * HALF
    starts = (
        (2 * (1 - t) + g) * width,
        (2 * (1 - t) + 1 - g) * width + HALF,
        (2 * t + g) * width,
        (2 * t + g) * width + HALF,
    )
    loads = [
        pltpu.make_async_copy(
            weight.at[:, pl.ds(pl.multiple_of(start, HEAD_DIM), HALF)], w_tiles.at[k], load_sem.at[2 + k]
        )
        for k, start in enumerate(starts)
    ]
    loads.append(pltpu.make_async_copy(residual.at[0, :, mine], res_own, load_sem.at[6]))
    loads.append(
        pltpu.make_async_copy(
            gate_table.at[:, pl.ds(pl.multiple_of((2 * t + g) * width, HEAD_DIM), width)], gate_rows, load_sem.at[7]
        )
    )
    for copy in loads:
        copy.start()

    def attend(i, b):
        start = ROWS * (1 - 2 // (1 + b) + 3 * (1 // (1 + b)))
        span = pl.ds(pl.multiple_of(start, ROWS), KEYS)
        scores = lax.dot_general(
            qb[i, block_rows(b), :], kb[i, span, :], (((1,), (1,)), ((), ())), preferred_element_type=F32
        )
        top = jnp.max(scores, axis=1, keepdims=True) * SCORE_SCALE
        high = top.astype(BF).astype(F32)
        low = (top - high).astype(BF).astype(F32)
        expo = jnp.exp2(scores * SCORE_SCALE - (high + low))
        total = jnp.sum(expo, axis=1, keepdims=True)
        summed = jnp.dot(expo.astype(BF), vb[i, span, :], preferred_element_type=F32)
        o_send[i, b, 0:ROWS, :] = summed.astype(BF)
        total_high = total.astype(BF).astype(F32)
        notes = jnp.zeros((NOTE, HEAD_DIM), F32)
        note_row = lax.broadcasted_iota(jnp.int32, (NOTE, HEAD_DIM), 0)
        for k, column in enumerate((high, low, total_high, total - total_high)):
            for part, (first, last) in enumerate(((0, HEAD_DIM), (HEAD_DIM, ROWS))):
                line = jnp.sum(jnp.where(same_lane(last - first), column[first:last], 0.0), axis=0, keepdims=True)
                notes = jnp.where(note_row == 4 * part + k, line, notes)
        o_send[i, b, ROWS:, :] = notes.astype(BF)

        block, core = b // 2, b % 2

        @pl.when(b == c)
        def _():
            pltpu.make_async_copy(
                o_send.at[i, b], o_recv.at[GROUP * c + i, 0], o_recv_sem.at[GROUP * c + i, 0]
            ).start()

        @pl.when(b != c)
        def _():
            place = (RING - block) % RING
            send(
                o_send.at[i, b],
                o_recv.at[GROUP * c + i, place],
                o_sem.at[i, b],
                o_recv_sem.at[GROUP * c + i, place],
                at(0, block, core),
            )

    def merge(head):
        for j in range(RING):
            await_bytes(o_recv.at[head, j], o_recv_sem.at[head, j])
        notes = [o_recv[head, j, ROWS:, :].astype(F32) for j in range(RING)]
        for part, (first, last) in enumerate(((0, HEAD_DIM), (HEAD_DIM, ROWS))):
            tops = [n[4 * part : 4 * part + 1] + n[4 * part + 1 : 4 * part + 2] for n in notes]
            totals = [n[4 * part + 2 : 4 * part + 3] + n[4 * part + 3 : 4 * part + 4] for n in notes]
            top = jnp.maximum(jnp.maximum(tops[0], tops[1]), jnp.maximum(tops[2], tops[3]))
            fades = [jnp.exp2(one - top) for one in tops]
            whole = fades[0] * totals[0] + fades[1] * totals[1] + fades[2] * totals[2] + fades[3] * totals[3]
            result = jnp.zeros((last - first, HEAD_DIM), F32)
            for j in range(RING):
                column = jnp.sum(
                    jnp.where(same_lane(last - first), fades[j] / whole, 0.0), axis=1, keepdims=True
                )
                result = result + o_recv[head, j, first:last, :].astype(F32) * column
            attn[head, first:last, :] = result.astype(BF)
        send(attn.at[head], attn_other.at[head], guide_send.at[head], guide_recv.at[head], (p, t, 1 - g))

    forward(0)
    send_own(2)

    @pl.loop(0, GROUP)
    def _(i):
        arrived(i)

        @pl.loop(0, 8)
        def _(n):
            @pl.when((n == 4) & (i < GROUP - 1))
            def _():
                forward(i + 1)

            @pl.when((n == 4) & (i < GROUP - 3))
            def _():
                send_own(i + 3)

            @pl.when((n == 6) & (i > 0))
            def _():
                merge(i - 1)
                merge(GROUP + i - 1)

            attend(i, (n + 4) % 8)

    merge(GROUP - 1)
    merge(2 * GROUP - 1)

    own_share = (GUIDE_SCALE - (2 * GUIDE_SCALE - 1) * g).astype(F32)
    other_share = (1.0 - GUIDE_SCALE + (2 * GUIDE_SCALE - 1) * g).astype(F32)

    @pl.loop(0, HEADS)
    def _(head):
        await_bytes(attn_other.at[head], guide_recv.at[head])
        both = own_share * attn[head].astype(F32) + other_share * attn_other[head].astype(F32)
        combined[:, head_columns(head)] = both.astype(BF)

    for copy in loads:
        copy.wait()

    neighbours = ((p, 1 - t, g), (p, 1 - t, 1 - g))
    for k in (0, 1):
        part_send[k] = jnp.dot(combined[...], w_tiles[k], preferred_element_type=F32).astype(BF)
        send(part_send.at[k], part_recv.at[k], part_send_sem.at[k], part_recv_sem.at[k], neighbours[k])
    for k in (0, 1):
        part_own[k] = jnp.dot(combined[...], w_tiles[2 + k], preferred_element_type=F32)
    await_bytes(res_other, res_sem.at[1])
    steps = lax.broadcasted_iota(jnp.int32, gate_rows.shape, 0)
    gate = jnp.sum(jnp.where(steps == timestep[0], gate_rows[...], 0.0), axis=0, keepdims=True)
    for k in (0, 1):
        columns = pl.ds(k * HALF, HALF)
        await_bytes(part_recv.at[k], part_recv_sem.at[k])
        base = own_share * res_own[:, columns].astype(F32) + other_share * res_other[:, columns].astype(F32)
        proj = part_own[k] + part_recv[k].astype(F32)
        out[:, columns] = (base + gate[:, k * HALF : (k + 1) * HALF] * proj).astype(BF)

    @pl.loop(0, GROUP)
    def _(i):
        for k in range(8):
            await_bytes(kb.at[i, block_rows(0), :], kv_sem.at[i, k])
        for k in range(4):
            await_bytes(q_rot.at[i], q_sem.at[i, k])
        await_bytes(kb.at[i, block_rows(2, 2), :], far_sem.at[i, 0])
        await_bytes(vb.at[i, block_rows(4, 2), :], far_sem.at[i, 1])
        await_bytes(qb.at[i, block_rows(6), :], far_sem.at[i, 2])
        await_bytes(qb.at[i, block_rows(3), :], far_sem.at[i, 3])
        for k in range(5):
            await_bytes(q_rot.at[i], sib_sem.at[i, k])

        @pl.loop(0, 8)
        def _(b):
            @pl.when(b != c)
            def _():
                await_bytes(o_send.at[i, b], o_sem.at[i, b])

    @pl.loop(0, HEADS)
    def _(head):
        await_bytes(attn.at[head], guide_send.at[head])

    await_bytes(res_other, res_sem.at[0])
    for k in (0, 1):
        await_bytes(part_send.at[k], part_send_sem.at[k])


def per_device(
    fresh_q, fresh_k, fresh_v, stale_k, stale_v, positions, residual, out_weight, gate_table, timestep
):
    width = 2 * HALF
    steps = gate_table.shape[0]
    in_hbm = pl.BlockSpec(memory_space=pl.ANY)
    in_vmem = pl.BlockSpec(memory_space=pltpu.VMEM)
    dma = pltpu.SemaphoreType.DMA
    return pl.pallas_call(
        kernel,
        out_shape=jax.ShapeDtypeStruct((ROWS, width), BF),
        in_specs=[in_hbm] * 8 + [in_vmem, in_vmem, pl.BlockSpec(memory_space=pltpu.SMEM)],
        out_specs=in_vmem,
        scratch_shapes=[
            pltpu.VMEM((GROUP, 10 * ROWS, HEAD_DIM), BF),
            pltpu.VMEM((GROUP, 10 * ROWS, HEAD_DIM), BF),
            pltpu.VMEM((GROUP, 8 * ROWS, HEAD_DIM), BF),
            pltpu.VMEM((ROWS, width), BF),
            pltpu.VMEM((ROWS, width), BF),
            pltpu.VMEM((HEADS, ROWS, HEAD_DIM), BF),
            pltpu.VMEM((HEADS, ROWS, HEAD_DIM), BF),
            pltpu.VMEM((GROUP, 8, ROWS + NOTE, HEAD_DIM), BF),
            pltpu.VMEM((HEADS, RING, ROWS + NOTE, HEAD_DIM), BF),
            pltpu.VMEM((HEADS, ROWS, HEAD_DIM), BF),
            pltpu.VMEM((HEADS, ROWS, HEAD_DIM), BF),
            pltpu.VMEM((ROWS, width), BF),
            pltpu.VMEM((4, width, HALF), BF),
            pltpu.VMEM((2, ROWS, HALF), BF),
            pltpu.VMEM((2, ROWS, HALF), BF),
            pltpu.VMEM((2, ROWS, HALF), F32),
            pltpu.VMEM((ROWS, width), BF),
            pltpu.VMEM((ROWS, width), BF),
            pltpu.VMEM((steps, width), F32),
            pltpu.VMEM((ROWS, HEAD_DIM), F32),
            pltpu.VMEM((ROWS, HEAD_DIM), F32),
            dma((KINDS * GROUP,)),
            dma((HEADS, RING)),
            dma((GROUP, 8)),
            dma((GROUP, 4)),
            dma((GROUP, 4)),
            dma((GROUP, 5)),
            dma((GROUP, 5)),
            dma((GROUP, 8)),
            dma((HEADS,)),
            dma((HEADS,)),
            dma((2,)),
            dma((2,)),
            dma((2,)),
            dma((8,)),
        ],
        compiler_params=pltpu.CompilerParams(
            collective_id=0, has_side_effects=True, vmem_limit_bytes=56 * 1024 * 1024
        ),
        cost_estimate=pl.CostEstimate(flops=8_000_000_000, bytes_accessed=12_000_000, transcendentals=12_000_000),
    )(
        fresh_q, fresh_k, fresh_v, stale_k, stale_v, residual, out_weight, gate_table,
        jnp.asarray(frequencies()), positions, timestep,
    )


def solution(mesh):
    in_specs = (
        P("guide", "patch", "tensor"),
        P("guide", "patch", "tensor"),
        P("guide", "patch", "tensor"),
        P("guide", "patch", "tensor"),
        P("guide", "patch", "tensor"),
        P(None, "patch"),
        P("guide", "patch", "tensor"),
        P("tensor", None),
        P(),
        P(),
    )
    out_specs = P("patch", ("tensor", "guide"))
    return jax.shard_map(per_device, mesh=mesh, in_specs=in_specs, out_specs=out_specs, check_vma=False)
```

```python
import functools
import math

import jax
import jax.numpy as jnp
import numpy as np
from jax import lax
from jax.experimental import pallas as pl
from jax.experimental.pallas import tpu as pltpu
from jax.sharding import PartitionSpec as P

MESH = pl.DeviceIdType.MESH
BF = jnp.bfloat16
F32 = jnp.float32
HEAD_DIM = 128
GUIDE_SCALE = 5.0
RING = 4
ROWS = 192
GROUP = 5
HEADS = 10
KEYS = 8 * ROWS
NOTE = 16
HALF = 640
SCORE_SCALE = math.log2(math.e) / math.sqrt(HEAD_DIM)

(K_LEFT, K_RIGHT, V_LEFT, V_RIGHT, K_FAR, V_FAR, Q_LEFT, Q_RIGHT, Q_FAR, SIB_K, SIB_V, SIB_FK, SIB_FV, SIB_Q) = range(14)
KINDS = 14


def frequencies():
    half_dim = HEAD_DIM // 2
    side_pairs = HEAD_DIM // 6
    frame_pairs = half_dim - 2 * side_pairs
    table = np.zeros((8, HEAD_DIM), np.float32)
    for pair in range(half_dim):
        if pair < frame_pairs:
            section, local, size = 0, pair, frame_pairs
        elif pair < frame_pairs + side_pairs:
            section, local, size = 1, pair - frame_pairs, side_pairs
        else:
            section, local, size = 2, pair - frame_pairs - side_pairs, side_pairs
        table[section, 2 * pair : 2 * pair + 2] = 10000.0 ** (-local / size)
    return table


def block_rows(index, count=1):
    return pl.ds(pl.multiple_of(index * ROWS, ROWS), count * ROWS)


def head_columns(head):
    return pl.ds(pl.multiple_of(head * HEAD_DIM, HEAD_DIM), HEAD_DIM)


def same_lane(rows):
    shape = (rows, HEAD_DIM)
    return lax.broadcasted_iota(jnp.int32, shape, 0) == lax.broadcasted_iota(jnp.int32, shape, 1)


def kernel(
    fresh_q, fresh_k, fresh_v, stale_k, stale_v, residual, weight, gate_table, freqs, positions, timestep,
    out,
    kb, vb, qb, q_raw, k_raw, q_rot, k_rot, o_send, o_recv, attn, attn_other, combined, w_tiles, part_send, part_recv,
    part_own, res_own, res_other, gate_rows, cosines, sines,
    recv, o_recv_sem, kv_sem, q_sem, far_sem, sib_sem, local_sem, o_sem, guide_send, guide_recv, part_send_sem,
    part_recv_sem, res_sem, load_sem,
):
    p, t, g = lax.axis_index("patch"), lax.axis_index("tensor"), lax.axis_index("guide")
    x, y, c = p // (2 * RING), (p // 2) % RING, p % 2
    sib = 1 - c

    def at(dx, dy, core):
        return (((x + dx) % RING * RING + (y + dy) % RING) * 2 + core, t, g)

    def send(src, dst, send_sem, recv_sem, device):
        pltpu.make_async_remote_copy(
            src_ref=src, dst_ref=dst, send_sem=send_sem, recv_sem=recv_sem, device_id=device, device_id_type=MESH
        ).start()

    def await_bytes(ref, sem):
        pltpu.make_async_copy(ref, ref, sem).wait()

    def got(kind, i):
        return recv.at[kind * GROUP + i]

    own_slot, fresh_slot = 1 + 7 * c, 9 - 9 * c

    load_q = pltpu.make_async_copy(fresh_q.at[0], q_raw, load_sem.at[0])
    load_k = pltpu.make_async_copy(fresh_k.at[0], k_raw, load_sem.at[1])
    load_q.start()
    load_k.start()

    peers = [at(dx, 0, core) for dx in (1, 3) for core in (0, 1)]
    peers += [at(0, dy, core) for dy in (1, 2, 3) for core in (0, 1)]
    peers += [at(0, 0, sib), (p, 1 - t, g), (p, 1 - t, 1 - g), (p, t, 1 - g)]
    barrier = pltpu.get_barrier_semaphore()
    for peer in peers:
        pl.semaphore_signal(barrier, inc=1, device_id=peer, device_id_type=MESH)

    def local_stale(i, start):
        columns = head_columns(GROUP * c + i)
        copies = (
            pltpu.make_async_copy(stale_k.at[0, :, columns], kb.at[i, block_rows(own_slot), :], local_sem.at[i, 0]),
            pltpu.make_async_copy(stale_v.at[0, :, columns], vb.at[i, block_rows(own_slot), :], local_sem.at[i, 1]),
            pltpu.make_async_copy(fresh_v.at[0, :, columns], vb.at[i, block_rows(fresh_slot), :], local_sem.at[i, 2]),
        )
        for copy in copies:
            copy.start() if start else copy.wait()

    def local_rotated(i, start):
        head = GROUP * c + i
        copies = (
            pltpu.make_async_copy(k_rot.at[head], kb.at[i, block_rows(fresh_slot), :], local_sem.at[i, 3]),
            pltpu.make_async_copy(q_rot.at[head], qb.at[i, block_rows(c), :], local_sem.at[i, 4]),
        )
        for copy in copies:
            copy.start() if start else copy.wait()

    def send_own(i, *cores):
        for core in cores or (0, 1):
            columns = head_columns(GROUP * core + i)
            for tensor, (source, buf) in enumerate(((stale_k, kb), (stale_v, vb))):
                for way, (dx, slot, kind) in enumerate(((1, 2, 2 * tensor), (3, 4, 2 * tensor + 1))):
                    send(
                        source.at[0, :, columns],
                        buf.at[i, block_rows(slot + c), :],
                        kv_sem.at[i, core * 4 + tensor * 2 + way],
                        got(kind, i),
                        at(dx, 0, core),
                    )

    def send_sibling_stale(i):
        columns = head_columns(GROUP * sib + i)
        device = at(0, 0, sib)
        send(stale_k.at[0, :, columns], kb.at[i, block_rows(own_slot), :], sib_sem.at[i, 0], got(SIB_K, i), device)
        send(stale_v.at[0, :, columns], vb.at[i, block_rows(own_slot), :], sib_sem.at[i, 1], got(SIB_V, i), device)
        send(fresh_v.at[0, :, columns], vb.at[i, block_rows(fresh_slot), :], sib_sem.at[i, 2], got(SIB_FV, i), device)

    def send_rotated(i):
        head = GROUP * sib + i
        device = at(0, 0, sib)
        send(q_rot.at[head], qb.at[i, block_rows(c), :], sib_sem.at[i, 3], got(SIB_Q, i), device)
        send(k_rot.at[head], kb.at[i, block_rows(fresh_slot), :], sib_sem.at[i, 4], got(SIB_FK, i), device)
        for core in (0, 1):
            for way, (dy, block, kind) in enumerate(((1, 6, Q_LEFT), (3, 2, Q_RIGHT))):
                send(
                    q_rot.at[GROUP * core + i],
                    qb.at[i, block_rows(block + c), :],
                    q_sem.at[i, core * 2 + way],
                    got(kind, i),
                    at(0, dy, core),
                )

    def forward(i):
        await_bytes(kb.at[i, block_rows(2, 2), :], got(K_LEFT, i))
        send(
            kb.at[i, block_rows(2, 2), :], kb.at[i, block_rows(6, 2), :], far_sem.at[i, 0], got(K_FAR, i), at(1, 0, c)
        )
        await_bytes(vb.at[i, block_rows(4, 2), :], got(V_RIGHT, i))
        send(
            vb.at[i, block_rows(4, 2), :], vb.at[i, block_rows(6, 2), :], far_sem.at[i, 1], got(V_FAR, i), at(3, 0, c)
        )
        await_bytes(qb.at[i, block_rows(6, 2), :], got(Q_LEFT, i))
        send(qb.at[i, block_rows(6), :], qb.at[i, block_rows(4), :], far_sem.at[i, 2], got(Q_FAR, i), at(0, 1, c))
        await_bytes(qb.at[i, block_rows(2, 2), :], got(Q_RIGHT, i))
        send(qb.at[i, block_rows(3), :], qb.at[i, block_rows(5), :], far_sem.at[i, 3], got(Q_FAR, i), at(0, 3, c))

    def arrived(i):
        local_stale(i, False)
        local_rotated(i, False)
        other = 8 - 7 * c
        other_fresh = 9 * c
        await_bytes(kb.at[i, block_rows(other), :], got(SIB_K, i))
        await_bytes(vb.at[i, block_rows(other), :], got(SIB_V, i))
        await_bytes(kb.at[i, block_rows(other_fresh), :], got(SIB_FK, i))
        await_bytes(vb.at[i, block_rows(other_fresh), :], got(SIB_FV, i))
        await_bytes(qb.at[i, block_rows(sib), :], got(SIB_Q, i))
        await_bytes(kb.at[i, block_rows(4, 2), :], got(K_RIGHT, i))
        await_bytes(vb.at[i, block_rows(2, 2), :], got(V_LEFT, i))
        await_bytes(kb.at[i, block_rows(6, 2), :], got(K_FAR, i))
        await_bytes(vb.at[i, block_rows(6, 2), :], got(V_FAR, i))
        await_bytes(qb.at[i, block_rows(4, 2), :], got(Q_FAR, i))

    @pl.loop(0, GROUP)
    def _(i):
        local_stale(i, True)

    res_columns = residual.shape[2] // 2
    mine = pl.ds(pl.multiple_of(g * res_columns, HEAD_DIM), res_columns)
    partner = pl.ds(pl.multiple_of((1 - g) * res_columns, HEAD_DIM), res_columns)

    where_at = positions[...].astype(F32)
    row_of = lax.broadcasted_iota(jnp.int32, (8, ROWS), 0)
    places = jnp.where(
        row_of == 0, where_at[0:1], jnp.where(row_of == 1, where_at[1:2], jnp.where(row_of == 2, where_at[2:3], 0.0))
    )
    angles = lax.dot_general(
        places, freqs[...], (((0,), (0,)), ((), ())), precision=lax.Precision.HIGHEST, preferred_element_type=F32
    )
    cosines[...] = jnp.cos(angles)
    sines[...] = jnp.sin(angles)
    row_ids = lax.broadcasted_iota(jnp.int32, (HEAD_DIM, HEAD_DIM), 0)
    col_ids = lax.broadcasted_iota(jnp.int32, (HEAD_DIM, HEAD_DIM), 1)
    swap = jnp.where(
        (row_ids % 2 == 1) & (col_ids == row_ids - 1),
        -1.0,
        jnp.where((row_ids % 2 == 0) & (col_ids == row_ids + 1), 1.0, 0.0),
    ).astype(BF)

    def rotated(raw, head):
        values = raw[:, head_columns(head)]
        turned = jnp.dot(values, swap, preferred_element_type=F32)
        return (values.astype(F32) * cosines[...] + turned * sines[...]).astype(BF)

    load_q.wait()
    load_k.wait()

    @pl.loop(0, GROUP)
    def _(i):
        for core in (0, 1):
            head = GROUP * core + i
            q_rot[head] = rotated(q_raw, head)
            k_rot[head] = rotated(k_raw, head)
        local_rotated(i, True)

    pl.semaphore_wait(barrier, len(peers))

    @pl.loop(0, GROUP)
    def _(i):
        @pl.when(i == 0)
        def _():
            send_own(0)

        send_rotated(i)
        send_sibling_stale(i)

    send_own(1, 0)

    send(residual.at[0, :, partner], res_other, res_sem.at[0], res_sem.at[1], (p, t, 1 - g))
    width = 2 * HALF
    starts = (
        (2 * (1 - t) + g) * width,
        (2 * (1 - t) + 1 - g) * width + HALF,
        (2 * t + g) * width,
        (2 * t + g) * width + HALF,
    )
    loads = [
        pltpu.make_async_copy(
            weight.at[:, pl.ds(pl.multiple_of(start, HEAD_DIM), HALF)], w_tiles.at[k], load_sem.at[2 + k]
        )
        for k, start in enumerate(starts)
    ]
    loads.append(pltpu.make_async_copy(residual.at[0, :, mine], res_own, load_sem.at[6]))
    loads.append(
        pltpu.make_async_copy(
            gate_table.at[:, pl.ds(pl.multiple_of((2 * t + g) * width, HEAD_DIM), width)], gate_rows, load_sem.at[7]
        )
    )
    for copy in loads:
        copy.start()

    def attend(i, b):
        start = ROWS * (1 - 2 // (1 + b) + 3 * (1 // (1 + b)))
        span = pl.ds(pl.multiple_of(start, ROWS), KEYS)
        scores = lax.dot_general(
            qb[i, block_rows(b), :], kb[i, span, :], (((1,), (1,)), ((), ())), preferred_element_type=F32
        )
        top = jnp.max(scores, axis=1, keepdims=True) * SCORE_SCALE
        high = top.astype(BF).astype(F32)
        low = (top - high).astype(BF).astype(F32)
        expo = jnp.exp2(scores * SCORE_SCALE - (high + low))
        total = jnp.sum(expo, axis=1, keepdims=True)
        summed = jnp.dot(expo.astype(BF), vb[i, span, :], preferred_element_type=F32)
        o_send[i, b, 0:ROWS, :] = summed.astype(BF)
        total_high = total.astype(BF).astype(F32)
        notes = jnp.zeros((NOTE, HEAD_DIM), F32)
        note_row = lax.broadcasted_iota(jnp.int32, (NOTE, HEAD_DIM), 0)
        for k, column in enumerate((high, low, total_high, total - total_high)):
            for part, (first, last) in enumerate(((0, HEAD_DIM), (HEAD_DIM, ROWS))):
                line = jnp.sum(jnp.where(same_lane(last - first), column[first:last], 0.0), axis=0, keepdims=True)
                notes = jnp.where(note_row == 4 * part + k, line, notes)
        o_send[i, b, ROWS:, :] = notes.astype(BF)

    def send_back(i, b):
        block, core = b // 2, b % 2

        @pl.when(b == c)
        def _():
            pltpu.make_async_copy(
                o_send.at[i, b], o_recv.at[GROUP * c + i, 0], o_recv_sem.at[GROUP * c + i, 0]
            ).start()

        @pl.when(b != c)
        def _():
            place = (RING - block) % RING
            send(
                o_send.at[i, b],
                o_recv.at[GROUP * c + i, place],
                o_sem.at[i, b],
                o_recv_sem.at[GROUP * c + i, place],
                at(0, block, core),
            )

    def merge(head):
        for j in range(RING):
            await_bytes(o_recv.at[head, j], o_recv_sem.at[head, j])
        notes = [o_recv[head, j, ROWS:, :].astype(F32) for j in range(RING)]
        for part, (first, last) in enumerate(((0, HEAD_DIM), (HEAD_DIM, ROWS))):
            tops = [n[4 * part : 4 * part + 1] + n[4 * part + 1 : 4 * part + 2] for n in notes]
            totals = [n[4 * part + 2 : 4 * part + 3] + n[4 * part + 3 : 4 * part + 4] for n in notes]
            top = jnp.maximum(jnp.maximum(tops[0], tops[1]), jnp.maximum(tops[2], tops[3]))
            fades = [jnp.exp2(one - top) for one in tops]
            whole = fades[0] * totals[0] + fades[1] * totals[1] + fades[2] * totals[2] + fades[3] * totals[3]
            result = jnp.zeros((last - first, HEAD_DIM), F32)
            for j in range(RING):
                column = jnp.sum(
                    jnp.where(same_lane(last - first), fades[j] / whole, 0.0), axis=1, keepdims=True
                )
                result = result + o_recv[head, j, first:last, :].astype(F32) * column
            attn[head, first:last, :] = result.astype(BF)
        send(attn.at[head], attn_other.at[head], guide_send.at[head], guide_recv.at[head], (p, t, 1 - g))

    forward(0)
    send_own(1, 1)
    send_own(2)

    @pl.loop(0, GROUP)
    def _(i):
        @pl.when(i < GROUP - 1)
        def _():
            forward(i + 1)

        @pl.when(i < GROUP - 3)
        def _():
            send_own(i + 3)

        arrived(i)

        @pl.loop(0, RING)
        def _(n):
            @pl.when((n == 3) & (i > 0))
            def _():
                merge(i - 1)
                merge(GROUP + i - 1)

            block = (n + 2) % RING
            attend(i, 2 * block)
            attend(i, 2 * block + 1)
            send_back(i, 2 * block)
            send_back(i, 2 * block + 1)

    merge(GROUP - 1)
    merge(2 * GROUP - 1)

    own_share = (GUIDE_SCALE - (2 * GUIDE_SCALE - 1) * g).astype(F32)
    other_share = (1.0 - GUIDE_SCALE + (2 * GUIDE_SCALE - 1) * g).astype(F32)

    @pl.loop(0, HEADS)
    def _(head):
        await_bytes(attn_other.at[head], guide_recv.at[head])
        both = own_share * attn[head].astype(F32) + other_share * attn_other[head].astype(F32)
        combined[:, head_columns(head)] = both.astype(BF)

    for copy in loads:
        copy.wait()

    neighbours = ((p, 1 - t, g), (p, 1 - t, 1 - g))
    for k in (0, 1):
        part_send[k] = jnp.dot(combined[...], w_tiles[k], preferred_element_type=F32).astype(BF)
        send(part_send.at[k], part_recv.at[k], part_send_sem.at[k], part_recv_sem.at[k], neighbours[k])
    for k in (0, 1):
        part_own[k] = jnp.dot(combined[...], w_tiles[2 + k], preferred_element_type=F32)
    await_bytes(res_other, res_sem.at[1])
    steps = lax.broadcasted_iota(jnp.int32, gate_rows.shape, 0)
    gate = jnp.sum(jnp.where(steps == timestep[0], gate_rows[...], 0.0), axis=0, keepdims=True)
    for k in (0, 1):
        columns = pl.ds(k * HALF, HALF)
        await_bytes(part_recv.at[k], part_recv_sem.at[k])
        base = own_share * res_own[:, columns].astype(F32) + other_share * res_other[:, columns].astype(F32)
        proj = part_own[k] + part_recv[k].astype(F32)
        out[:, columns] = (base + gate[:, k * HALF : (k + 1) * HALF] * proj).astype(BF)

    @pl.loop(0, GROUP)
    def _(i):
        for k in range(8):
            await_bytes(kb.at[i, block_rows(0), :], kv_sem.at[i, k])
        for k in range(4):
            await_bytes(q_rot.at[i], q_sem.at[i, k])
        await_bytes(kb.at[i, block_rows(2, 2), :], far_sem.at[i, 0])
        await_bytes(vb.at[i, block_rows(4, 2), :], far_sem.at[i, 1])
        await_bytes(qb.at[i, block_rows(6), :], far_sem.at[i, 2])
        await_bytes(qb.at[i, block_rows(3), :], far_sem.at[i, 3])
        for k in range(5):
            await_bytes(q_rot.at[i], sib_sem.at[i, k])

        @pl.loop(0, 8)
        def _(b):
            @pl.when(b != c)
            def _():
                await_bytes(o_send.at[i, b], o_sem.at[i, b])

    @pl.loop(0, HEADS)
    def _(head):
        await_bytes(attn.at[head], guide_send.at[head])

    await_bytes(res_other, res_sem.at[0])
    for k in (0, 1):
        await_bytes(part_send.at[k], part_send_sem.at[k])


def per_device(
    fresh_q, fresh_k, fresh_v, stale_k, stale_v, positions, residual, out_weight, gate_table, timestep
):
    width = 2 * HALF
    steps = gate_table.shape[0]
    in_hbm = pl.BlockSpec(memory_space=pl.ANY)
    in_vmem = pl.BlockSpec(memory_space=pltpu.VMEM)
    dma = pltpu.SemaphoreType.DMA
    return pl.pallas_call(
        kernel,
        out_shape=jax.ShapeDtypeStruct((ROWS, width), BF),
        in_specs=[in_hbm] * 8 + [in_vmem, in_vmem, pl.BlockSpec(memory_space=pltpu.SMEM)],
        out_specs=in_vmem,
        scratch_shapes=[
            pltpu.VMEM((GROUP, 10 * ROWS, HEAD_DIM), BF),
            pltpu.VMEM((GROUP, 10 * ROWS, HEAD_DIM), BF),
            pltpu.VMEM((GROUP, 8 * ROWS, HEAD_DIM), BF),
            pltpu.VMEM((ROWS, width), BF),
            pltpu.VMEM((ROWS, width), BF),
            pltpu.VMEM((HEADS, ROWS, HEAD_DIM), BF),
            pltpu.VMEM((HEADS, ROWS, HEAD_DIM), BF),
            pltpu.VMEM((GROUP, 8, ROWS + NOTE, HEAD_DIM), BF),
            pltpu.VMEM((HEADS, RING, ROWS + NOTE, HEAD_DIM), BF),
            pltpu.VMEM((HEADS, ROWS, HEAD_DIM), BF),
            pltpu.VMEM((HEADS, ROWS, HEAD_DIM), BF),
            pltpu.VMEM((ROWS, width), BF),
            pltpu.VMEM((4, width, HALF), BF),
            pltpu.VMEM((2, ROWS, HALF), BF),
            pltpu.VMEM((2, ROWS, HALF), BF),
            pltpu.VMEM((2, ROWS, HALF), F32),
            pltpu.VMEM((ROWS, width), BF),
            pltpu.VMEM((ROWS, width), BF),
            pltpu.VMEM((steps, width), F32),
            pltpu.VMEM((ROWS, HEAD_DIM), F32),
            pltpu.VMEM((ROWS, HEAD_DIM), F32),
            dma((KINDS * GROUP,)),
            dma((HEADS, RING)),
            dma((GROUP, 8)),
            dma((GROUP, 4)),
            dma((GROUP, 4)),
            dma((GROUP, 5)),
            dma((GROUP, 5)),
            dma((GROUP, 8)),
            dma((HEADS,)),
            dma((HEADS,)),
            dma((2,)),
            dma((2,)),
            dma((2,)),
            dma((8,)),
        ],
        compiler_params=pltpu.CompilerParams(
            collective_id=0, has_side_effects=True, vmem_limit_bytes=56 * 1024 * 1024
        ),
        cost_estimate=pl.CostEstimate(flops=8_000_000_000, bytes_accessed=12_000_000, transcendentals=12_000_000),
    )(
        fresh_q, fresh_k, fresh_v, stale_k, stale_v, residual, out_weight, gate_table,
        jnp.asarray(frequencies()), positions, timestep,
    )


def solution(mesh):
    in_specs = (
        P("guide", "patch", "tensor"),
        P("guide", "patch", "tensor"),
        P("guide", "patch", "tensor"),
        P("guide", "patch", "tensor"),
        P("guide", "patch", "tensor"),
        P(None, "patch"),
        P("guide", "patch", "tensor"),
        P("tensor", None),
        P(),
        P(),
    )
    out_specs = P("patch", ("tensor", "guide"))
    return jax.shard_map(per_device, mesh=mesh, in_specs=in_specs, out_specs=out_specs, check_vma=False)
```

```python
import functools
import math

import jax
import jax.numpy as jnp
import numpy as np
from jax import lax
from jax.experimental import pallas as pl
from jax.experimental.pallas import tpu as pltpu
from jax.sharding import PartitionSpec as P

MESH = pl.DeviceIdType.MESH
BF = jnp.bfloat16
F32 = jnp.float32
HEAD_DIM = 128
GUIDE_SCALE = 5.0
RING = 4
ROWS = 192
GROUP = 5
HEADS = 10
KEYS = 8 * ROWS
NOTE = 16
HALF = 640
SCORE_SCALE = math.log2(math.e) / math.sqrt(HEAD_DIM)

(K_LEFT, K_RIGHT, V_LEFT, V_RIGHT, K_FAR, V_FAR, Q_LEFT, Q_RIGHT, Q_FAR, SIB_K, SIB_V, SIB_FK, SIB_FV, SIB_Q) = range(14)
KINDS = 14


def frequencies():
    half_dim = HEAD_DIM // 2
    side_pairs = HEAD_DIM // 6
    frame_pairs = half_dim - 2 * side_pairs
    table = np.zeros((8, HEAD_DIM), np.float32)
    for pair in range(half_dim):
        if pair < frame_pairs:
            section, local, size = 0, pair, frame_pairs
        elif pair < frame_pairs + side_pairs:
            section, local, size = 1, pair - frame_pairs, side_pairs
        else:
            section, local, size = 2, pair - frame_pairs - side_pairs, side_pairs
        table[section, 2 * pair : 2 * pair + 2] = 10000.0 ** (-local / size)
    return table


def block_rows(index, count=1):
    return pl.ds(pl.multiple_of(index * ROWS, ROWS), count * ROWS)


def head_columns(head):
    return pl.ds(pl.multiple_of(head * HEAD_DIM, HEAD_DIM), HEAD_DIM)


def same_lane(rows):
    shape = (rows, HEAD_DIM)
    return lax.broadcasted_iota(jnp.int32, shape, 0) == lax.broadcasted_iota(jnp.int32, shape, 1)


def kernel(
    fresh_q, fresh_k, fresh_v, stale_k, stale_v, residual, weight, gate_table, freqs, positions, timestep,
    out,
    kb, vb, qb, scores_a, scores_b, weights_a, weights_b, q_raw, k_raw, q_rot, k_rot, o_send, o_recv, attn, attn_other, combined, w_tiles, part_send, part_recv,
    part_own, res_own, res_other, gate_rows, cosines, sines,
    recv, o_recv_sem, kv_sem, q_sem, far_sem, sib_sem, local_sem, o_sem, guide_send, guide_recv, part_send_sem,
    part_recv_sem, res_sem, load_sem,
):
    p, t, g = lax.axis_index("patch"), lax.axis_index("tensor"), lax.axis_index("guide")
    x, y, c = p // (2 * RING), (p // 2) % RING, p % 2
    sib = 1 - c

    def at(dx, dy, core):
        return (((x + dx) % RING * RING + (y + dy) % RING) * 2 + core, t, g)

    def send(src, dst, send_sem, recv_sem, device):
        pltpu.make_async_remote_copy(
            src_ref=src, dst_ref=dst, send_sem=send_sem, recv_sem=recv_sem, device_id=device, device_id_type=MESH
        ).start()

    def await_bytes(ref, sem):
        pltpu.make_async_copy(ref, ref, sem).wait()

    def got(kind, i):
        return recv.at[kind * GROUP + i]

    own_slot, fresh_slot = 1 + 7 * c, 9 - 9 * c

    load_q = pltpu.make_async_copy(fresh_q.at[0], q_raw, load_sem.at[0])
    load_k = pltpu.make_async_copy(fresh_k.at[0], k_raw, load_sem.at[1])
    load_q.start()
    load_k.start()

    peers = [at(dx, 0, core) for dx in (1, 3) for core in (0, 1)]
    peers += [at(0, dy, core) for dy in (1, 2, 3) for core in (0, 1)]
    peers += [at(0, 0, sib), (p, 1 - t, g), (p, 1 - t, 1 - g), (p, t, 1 - g)]
    barrier = pltpu.get_barrier_semaphore()
    for peer in peers:
        pl.semaphore_signal(barrier, inc=1, device_id=peer, device_id_type=MESH)

    def local_stale(i, start):
        columns = head_columns(GROUP * c + i)
        copies = (
            pltpu.make_async_copy(stale_k.at[0, :, columns], kb.at[i, block_rows(own_slot), :], local_sem.at[i, 0]),
            pltpu.make_async_copy(stale_v.at[0, :, columns], vb.at[i, block_rows(own_slot), :], local_sem.at[i, 1]),
            pltpu.make_async_copy(fresh_v.at[0, :, columns], vb.at[i, block_rows(fresh_slot), :], local_sem.at[i, 2]),
        )
        for copy in copies:
            copy.start() if start else copy.wait()

    def local_rotated(i, start):
        head = GROUP * c + i
        copies = (
            pltpu.make_async_copy(k_rot.at[head], kb.at[i, block_rows(fresh_slot), :], local_sem.at[i, 3]),
            pltpu.make_async_copy(q_rot.at[head], qb.at[i, block_rows(c), :], local_sem.at[i, 4]),
        )
        for copy in copies:
            copy.start() if start else copy.wait()

    def send_own(i, *cores):
        for core in cores or (0, 1):
            columns = head_columns(GROUP * core + i)
            for tensor, (source, buf) in enumerate(((stale_k, kb), (stale_v, vb))):
                for way, (dx, slot, kind) in enumerate(((1, 2, 2 * tensor), (3, 4, 2 * tensor + 1))):
                    send(
                        source.at[0, :, columns],
                        buf.at[i, block_rows(slot + c), :],
                        kv_sem.at[i, core * 4 + tensor * 2 + way],
                        got(kind, i),
                        at(dx, 0, core),
                    )

    def send_sibling_stale(i):
        columns = head_columns(GROUP * sib + i)
        device = at(0, 0, sib)
        send(stale_k.at[0, :, columns], kb.at[i, block_rows(own_slot), :], sib_sem.at[i, 0], got(SIB_K, i), device)
        send(stale_v.at[0, :, columns], vb.at[i, block_rows(own_slot), :], sib_sem.at[i, 1], got(SIB_V, i), device)
        send(fresh_v.at[0, :, columns], vb.at[i, block_rows(fresh_slot), :], sib_sem.at[i, 2], got(SIB_FV, i), device)

    def send_rotated(i):
        head = GROUP * sib + i
        device = at(0, 0, sib)
        send(q_rot.at[head], qb.at[i, block_rows(c), :], sib_sem.at[i, 3], got(SIB_Q, i), device)
        send(k_rot.at[head], kb.at[i, block_rows(fresh_slot), :], sib_sem.at[i, 4], got(SIB_FK, i), device)

    def send_queries(i):
        for core in (0, 1):
            for way, (dy, block, kind) in enumerate(((1, 6, Q_LEFT), (3, 2, Q_RIGHT))):
                send(
                    q_rot.at[GROUP * core + i],
                    qb.at[i, block_rows(block + c), :],
                    q_sem.at[i, core * 2 + way],
                    got(kind, i),
                    at(0, dy, core),
                )

    def forward_queries(i):
        await_bytes(qb.at[i, block_rows(6, 2), :], got(Q_LEFT, i))
        send(qb.at[i, block_rows(6), :], qb.at[i, block_rows(4), :], far_sem.at[i, 2], got(Q_FAR, i), at(0, 1, c))
        await_bytes(qb.at[i, block_rows(2, 2), :], got(Q_RIGHT, i))
        send(qb.at[i, block_rows(3), :], qb.at[i, block_rows(5), :], far_sem.at[i, 3], got(Q_FAR, i), at(0, 3, c))

    def forward_keys(i):
        await_bytes(kb.at[i, block_rows(2, 2), :], got(K_LEFT, i))
        send(
            kb.at[i, block_rows(2, 2), :], kb.at[i, block_rows(6, 2), :], far_sem.at[i, 0], got(K_FAR, i), at(1, 0, c)
        )
        await_bytes(vb.at[i, block_rows(4, 2), :], got(V_RIGHT, i))
        send(
            vb.at[i, block_rows(4, 2), :], vb.at[i, block_rows(6, 2), :], far_sem.at[i, 1], got(V_FAR, i), at(3, 0, c)
        )

    def arrived(i):
        local_stale(i, False)
        local_rotated(i, False)
        other = 8 - 7 * c
        other_fresh = 9 * c
        await_bytes(kb.at[i, block_rows(other), :], got(SIB_K, i))
        await_bytes(vb.at[i, block_rows(other), :], got(SIB_V, i))
        await_bytes(kb.at[i, block_rows(other_fresh), :], got(SIB_FK, i))
        await_bytes(vb.at[i, block_rows(other_fresh), :], got(SIB_FV, i))
        await_bytes(qb.at[i, block_rows(sib), :], got(SIB_Q, i))
        await_bytes(kb.at[i, block_rows(4, 2), :], got(K_RIGHT, i))
        await_bytes(vb.at[i, block_rows(2, 2), :], got(V_LEFT, i))
        await_bytes(kb.at[i, block_rows(6, 2), :], got(K_FAR, i))
        await_bytes(vb.at[i, block_rows(6, 2), :], got(V_FAR, i))
        await_bytes(qb.at[i, block_rows(4, 2), :], got(Q_FAR, i))

    @pl.loop(0, GROUP)
    def _(i):
        local_stale(i, True)

    res_columns = residual.shape[2] // 2
    mine = pl.ds(pl.multiple_of(g * res_columns, HEAD_DIM), res_columns)
    partner = pl.ds(pl.multiple_of((1 - g) * res_columns, HEAD_DIM), res_columns)

    where_at = positions[...].astype(F32)
    row_of = lax.broadcasted_iota(jnp.int32, (8, ROWS), 0)
    places = jnp.where(
        row_of == 0, where_at[0:1], jnp.where(row_of == 1, where_at[1:2], jnp.where(row_of == 2, where_at[2:3], 0.0))
    )
    angles = lax.dot_general(
        places, freqs[...], (((0,), (0,)), ((), ())), precision=lax.Precision.HIGHEST, preferred_element_type=F32
    )
    cosines[...] = jnp.cos(angles)
    sines[...] = jnp.sin(angles)
    row_ids = lax.broadcasted_iota(jnp.int32, (HEAD_DIM, HEAD_DIM), 0)
    col_ids = lax.broadcasted_iota(jnp.int32, (HEAD_DIM, HEAD_DIM), 1)
    swap = jnp.where(
        (row_ids % 2 == 1) & (col_ids == row_ids - 1),
        -1.0,
        jnp.where((row_ids % 2 == 0) & (col_ids == row_ids + 1), 1.0, 0.0),
    ).astype(BF)

    def rotated(raw, head):
        values = raw[:, head_columns(head)]
        turned = jnp.dot(values, swap, preferred_element_type=F32)
        return (values.astype(F32) * cosines[...] + turned * sines[...]).astype(BF)

    load_q.wait()
    load_k.wait()

    @pl.loop(0, GROUP)
    def _(i):
        for core in (0, 1):
            head = GROUP * core + i
            q_rot[head] = rotated(q_raw, head)
            k_rot[head] = rotated(k_raw, head)
        local_rotated(i, True)

    pl.semaphore_wait(barrier, len(peers))

    send_own(0)
    send_queries(0)

    @pl.loop(0, GROUP)
    def _(i):
        send_sibling_stale(i)
        send_rotated(i)

    send_own(1, 0)
    send_queries(1)

    send(residual.at[0, :, partner], res_other, res_sem.at[0], res_sem.at[1], (p, t, 1 - g))
    width = 2 * HALF
    starts = (
        (2 * (1 - t) + g) * width,
        (2 * (1 - t) + 1 - g) * width + HALF,
        (2 * t + g) * width,
        (2 * t + g) * width + HALF,
    )
    loads = [
        pltpu.make_async_copy(
            weight.at[:, pl.ds(pl.multiple_of(start, HEAD_DIM), HALF)], w_tiles.at[k], load_sem.at[2 + k]
        )
        for k, start in enumerate(starts)
    ]
    loads.append(pltpu.make_async_copy(residual.at[0, :, mine], res_own, load_sem.at[6]))
    loads.append(
        pltpu.make_async_copy(
            gate_table.at[:, pl.ds(pl.multiple_of((2 * t + g) * width, HEAD_DIM), width)], gate_rows, load_sem.at[7]
        )
    )
    for copy in loads:
        copy.start()

    def pieces(chip):
        if chip:
            return [(0, 2 * ROWS, ROWS)]
        return [(0, ROWS, 2 * ROWS), (ROWS, 2 * ROWS, 0)]

    def score(i, chip, scores):
        for first, last, keys in pieces(chip):
            scores[first:last, :] = lax.dot_general(
                qb[i, 2 * chip * ROWS + first : 2 * chip * ROWS + last, :],
                kb[i, keys : keys + KEYS, :],
                (((1,), (1,)), ((), ())),
                preferred_element_type=F32,
            )

    def soften(i, chip, scores, weights):
        for half in (0, 1):
            rows = slice(half * ROWS, (half + 1) * ROWS)
            top = jnp.max(scores[rows, :], axis=1, keepdims=True) * SCORE_SCALE
            expo = jnp.exp2(scores[rows, :] * SCORE_SCALE - top)
            total = jnp.sum(expo, axis=1, keepdims=True)
            weights[rows, :] = expo.astype(BF)
            notes = jnp.zeros((NOTE, HEAD_DIM), F32)
            note_row = lax.broadcasted_iota(jnp.int32, (NOTE, HEAD_DIM), 0)
            for part, (first, last) in enumerate(((0, HEAD_DIM), (HEAD_DIM, ROWS))):
                for k, (column, count) in enumerate(((top, 3), (total, 2))):
                    rest = jnp.sum(jnp.where(same_lane(last - first), column[first:last], 0.0), axis=0, keepdims=True)
                    for piece in range(count):
                        line = rest.astype(BF).astype(F32)
                        rest = rest - line
                        notes = jnp.where(note_row == 8 * part + 3 * k + piece, line, notes)
            o_send[i, 2 * chip + half, ROWS:, :] = notes.astype(BF)

    def weigh(i, chip, weights):
        for first, last, keys in pieces(chip):
            summed = jnp.dot(
                weights[first:last, :], vb[i, keys : keys + KEYS, :], preferred_element_type=F32
            ).astype(BF)
            for row in range(first, last, ROWS):
                o_send[i, 2 * chip + row // ROWS, 0:ROWS, :] = summed[row - first : row - first + ROWS]

    def send_back(i, b):
        block, core = b // 2, b % 2

        def away():
            place = (RING - block) % RING
            send(
                o_send.at[i, b],
                o_recv.at[GROUP * c + i, place],
                o_sem.at[i, b],
                o_recv_sem.at[GROUP * c + i, place],
                at(0, block, core),
            )

        if block:
            away()
        else:
            pl.when(core != c)(away)

            @pl.when(core == c)
            def _():
                pltpu.make_async_copy(
                    o_send.at[i, b], o_recv.at[GROUP * c + i, 0], o_recv_sem.at[GROUP * c + i, 0]
                ).start()

    def merge(head):
        for j in range(RING):
            await_bytes(o_recv.at[head, j], o_recv_sem.at[head, j])
        notes = [o_recv[head, j, ROWS:, :].astype(F32) for j in range(RING)]
        for part, (first, last) in enumerate(((0, HEAD_DIM), (HEAD_DIM, ROWS))):
            lines = [[n[8 * part + k : 8 * part + k + 1] for k in range(5)] for n in notes]
            tops = [line[0] + line[1] + line[2] for line in lines]
            totals = [line[3] + line[4] for line in lines]
            top = jnp.maximum(jnp.maximum(tops[0], tops[1]), jnp.maximum(tops[2], tops[3]))
            fades = [jnp.exp2(one - top) for one in tops]
            whole = fades[0] * totals[0] + fades[1] * totals[1] + fades[2] * totals[2] + fades[3] * totals[3]
            result = jnp.zeros((last - first, HEAD_DIM), F32)
            for j in range(RING):
                column = jnp.sum(
                    jnp.where(same_lane(last - first), fades[j] / whole, 0.0), axis=1, keepdims=True
                )
                result = result + o_recv[head, j, first:last, :].astype(F32) * column
            attn[head, first:last, :] = result.astype(BF)
        send(attn.at[head], attn_other.at[head], guide_send.at[head], guide_recv.at[head], (p, t, 1 - g))

    forward_queries(0)
    send_queries(2)
    forward_keys(0)
    send_own(1, 1)
    send_own(2)

    @pl.loop(0, GROUP)
    def _(i):
        @pl.when(i < GROUP - 1)
        def _():
            forward_queries(i + 1)
            forward_keys(i + 1)

        @pl.when(i < GROUP - 3)
        def _():
            send_queries(i + 3)
            send_own(i + 3)

        arrived(i)

        order = (2, 3, 1, 0)
        scores = (scores_a, scores_b)
        weights = (weights_a, weights_b)
        for n in range(len(order) + 2):
            if n >= 2:
                weigh(i, order[n - 2], weights[n % 2])
            if n < len(order):
                score(i, order[n], scores[n % 2])
            if 1 <= n <= len(order):
                soften(i, order[n - 1], scores[(n - 1) % 2], weights[(n - 1) % 2])
            if n >= 2:
                send_back(i, 2 * order[n - 2])
                send_back(i, 2 * order[n - 2] + 1)

        @pl.when(i > 0)
        def _():
            merge(i - 1)
            merge(GROUP + i - 1)

    merge(GROUP - 1)
    merge(2 * GROUP - 1)

    own_share = (GUIDE_SCALE - (2 * GUIDE_SCALE - 1) * g).astype(F32)
    other_share = (1.0 - GUIDE_SCALE + (2 * GUIDE_SCALE - 1) * g).astype(F32)

    @pl.loop(0, HEADS)
    def _(head):
        await_bytes(attn_other.at[head], guide_recv.at[head])
        both = own_share * attn[head].astype(F32) + other_share * attn_other[head].astype(F32)
        combined[:, head_columns(head)] = both.astype(BF)

    for copy in loads:
        copy.wait()

    neighbours = ((p, 1 - t, g), (p, 1 - t, 1 - g))
    for k in (0, 1):
        part_send[k] = jnp.dot(combined[...], w_tiles[k], preferred_element_type=F32).astype(BF)
        send(part_send.at[k], part_recv.at[k], part_send_sem.at[k], part_recv_sem.at[k], neighbours[k])
    for k in (0, 1):
        part_own[k] = jnp.dot(combined[...], w_tiles[2 + k], preferred_element_type=F32)
    await_bytes(res_other, res_sem.at[1])
    steps = lax.broadcasted_iota(jnp.int32, gate_rows.shape, 0)
    gate = jnp.sum(jnp.where(steps == timestep[0], gate_rows[...], 0.0), axis=0, keepdims=True)
    for k in (0, 1):
        columns = pl.ds(k * HALF, HALF)
        await_bytes(part_recv.at[k], part_recv_sem.at[k])
        base = own_share * res_own[:, columns].astype(F32) + other_share * res_other[:, columns].astype(F32)
        proj = part_own[k] + part_recv[k].astype(F32)
        out[:, columns] = (base + gate[:, k * HALF : (k + 1) * HALF] * proj).astype(BF)

    @pl.loop(0, GROUP)
    def _(i):
        for k in range(8):
            await_bytes(kb.at[i, block_rows(0), :], kv_sem.at[i, k])
        for k in range(4):
            await_bytes(q_rot.at[i], q_sem.at[i, k])
        await_bytes(kb.at[i, block_rows(2, 2), :], far_sem.at[i, 0])
        await_bytes(vb.at[i, block_rows(4, 2), :], far_sem.at[i, 1])
        await_bytes(qb.at[i, block_rows(6), :], far_sem.at[i, 2])
        await_bytes(qb.at[i, block_rows(3), :], far_sem.at[i, 3])
        for k in range(5):
            await_bytes(q_rot.at[i], sib_sem.at[i, k])

        @pl.loop(0, 8)
        def _(b):
            @pl.when(b != c)
            def _():
                await_bytes(o_send.at[i, b], o_sem.at[i, b])

    @pl.loop(0, HEADS)
    def _(head):
        await_bytes(attn.at[head], guide_send.at[head])

    await_bytes(res_other, res_sem.at[0])
    for k in (0, 1):
        await_bytes(part_send.at[k], part_send_sem.at[k])


def per_device(
    fresh_q, fresh_k, fresh_v, stale_k, stale_v, positions, residual, out_weight, gate_table, timestep
):
    width = 2 * HALF
    steps = gate_table.shape[0]
    in_hbm = pl.BlockSpec(memory_space=pl.ANY)
    in_vmem = pl.BlockSpec(memory_space=pltpu.VMEM)
    dma = pltpu.SemaphoreType.DMA
    return pl.pallas_call(
        kernel,
        out_shape=jax.ShapeDtypeStruct((ROWS, width), BF),
        in_specs=[in_hbm] * 8 + [in_vmem, in_vmem, pl.BlockSpec(memory_space=pltpu.SMEM)],
        out_specs=in_vmem,
        scratch_shapes=[
            pltpu.VMEM((GROUP, 10 * ROWS, HEAD_DIM), BF),
            pltpu.VMEM((GROUP, 10 * ROWS, HEAD_DIM), BF),
            pltpu.VMEM((GROUP, 8 * ROWS, HEAD_DIM), BF),
            pltpu.VMEM((2 * ROWS, KEYS), F32),
            pltpu.VMEM((2 * ROWS, KEYS), F32),
            pltpu.VMEM((2 * ROWS, KEYS), BF),
            pltpu.VMEM((2 * ROWS, KEYS), BF),
            pltpu.VMEM((ROWS, width), BF),
            pltpu.VMEM((ROWS, width), BF),
            pltpu.VMEM((HEADS, ROWS, HEAD_DIM), BF),
            pltpu.VMEM((HEADS, ROWS, HEAD_DIM), BF),
            pltpu.VMEM((GROUP, 8, ROWS + NOTE, HEAD_DIM), BF),
            pltpu.VMEM((HEADS, RING, ROWS + NOTE, HEAD_DIM), BF),
            pltpu.VMEM((HEADS, ROWS, HEAD_DIM), BF),
            pltpu.VMEM((HEADS, ROWS, HEAD_DIM), BF),
            pltpu.VMEM((ROWS, width), BF),
            pltpu.VMEM((4, width, HALF), BF),
            pltpu.VMEM((2, ROWS, HALF), BF),
            pltpu.VMEM((2, ROWS, HALF), BF),
            pltpu.VMEM((2, ROWS, HALF), F32),
            pltpu.VMEM((ROWS, width), BF),
            pltpu.VMEM((ROWS, width), BF),
            pltpu.VMEM((steps, width), F32),
            pltpu.VMEM((ROWS, HEAD_DIM), F32),
            pltpu.VMEM((ROWS, HEAD_DIM), F32),
            dma((KINDS * GROUP,)),
            dma((HEADS, RING)),
            dma((GROUP, 8)),
            dma((GROUP, 4)),
            dma((GROUP, 4)),
            dma((GROUP, 5)),
            dma((GROUP, 5)),
            dma((GROUP, 8)),
            dma((HEADS,)),
            dma((HEADS,)),
            dma((2,)),
            dma((2,)),
            dma((2,)),
            dma((8,)),
        ],
        compiler_params=pltpu.CompilerParams(
            collective_id=0, has_side_effects=True, vmem_limit_bytes=56 * 1024 * 1024
        ),
        cost_estimate=pl.CostEstimate(flops=8_000_000_000, bytes_accessed=12_000_000, transcendentals=12_000_000),
    )(
        fresh_q, fresh_k, fresh_v, stale_k, stale_v, residual, out_weight, gate_table,
        jnp.asarray(frequencies()), positions, timestep,
    )


def solution(mesh):
    in_specs = (
        P("guide", "patch", "tensor"),
        P("guide", "patch", "tensor"),
        P("guide", "patch", "tensor"),
        P("guide", "patch", "tensor"),
        P("guide", "patch", "tensor"),
        P(None, "patch"),
        P("guide", "patch", "tensor"),
        P("tensor", None),
        P(),
        P(),
    )
    out_specs = P("patch", ("tensor", "guide"))
    return jax.shard_map(per_device, mesh=mesh, in_specs=in_specs, out_specs=out_specs, check_vma=False)
```

```python
import functools
import math

import jax
import jax.numpy as jnp
import numpy as np
from jax import lax
from jax.experimental import pallas as pl
from jax.experimental.pallas import tpu as pltpu
from jax.sharding import PartitionSpec as P

MESH = pl.DeviceIdType.MESH
BF = jnp.bfloat16
F32 = jnp.float32
HEAD_DIM = 128
GUIDE_SCALE = 5.0
RING = 4
ROWS = 192
GROUP = 5
HEADS = 10
KEYS = 8 * ROWS
NOTE = 16
HALF = 640
SCORE_SCALE = math.log2(math.e) / math.sqrt(HEAD_DIM)

(K_LEFT, K_RIGHT, V_LEFT, V_RIGHT, K_FAR, V_FAR, Q_LEFT, Q_RIGHT, Q_FAR, SIB_K, SIB_V, SIB_FK, SIB_FV, SIB_Q) = range(14)
KINDS = 14


def frequencies():
    half_dim = HEAD_DIM // 2
    side_pairs = HEAD_DIM // 6
    frame_pairs = half_dim - 2 * side_pairs
    table = np.zeros((8, HEAD_DIM), np.float32)
    for pair in range(half_dim):
        if pair < frame_pairs:
            section, local, size = 0, pair, frame_pairs
        elif pair < frame_pairs + side_pairs:
            section, local, size = 1, pair - frame_pairs, side_pairs
        else:
            section, local, size = 2, pair - frame_pairs - side_pairs, side_pairs
        table[section, 2 * pair : 2 * pair + 2] = 10000.0 ** (-local / size)
    return table


def block_rows(index, count=1):
    return pl.ds(pl.multiple_of(index * ROWS, ROWS), count * ROWS)


def head_columns(head):
    return pl.ds(pl.multiple_of(head * HEAD_DIM, HEAD_DIM), HEAD_DIM)


def same_lane(rows):
    shape = (rows, HEAD_DIM)
    return lax.broadcasted_iota(jnp.int32, shape, 0) == lax.broadcasted_iota(jnp.int32, shape, 1)


def kernel(
    fresh_q, fresh_k, fresh_v, stale_k, stale_v, residual, weight, gate_table, freqs, positions, timestep,
    out,
    kb, vb, qb, scores_a, scores_b, weights_a, weights_b, q_raw, k_raw, q_rot, k_rot, o_send, o_recv, attn, attn_other, combined, w_tiles, part_send, part_recv,
    part, base, res_own, res_other, gate_rows, cosines, sines,
    recv, o_recv_sem, kv_sem, q_sem, far_sem, sib_sem, local_sem, o_sem, guide_send, guide_recv, part_send_sem,
    part_recv_sem, res_sem, load_sem,
):
    p, t, g = lax.axis_index("patch"), lax.axis_index("tensor"), lax.axis_index("guide")
    x, y, c = p // (2 * RING), (p // 2) % RING, p % 2
    sib = 1 - c

    def at(dx, dy, core):
        return (((x + dx) % RING * RING + (y + dy) % RING) * 2 + core, t, g)

    def send(src, dst, send_sem, recv_sem, device):
        pltpu.make_async_remote_copy(
            src_ref=src, dst_ref=dst, send_sem=send_sem, recv_sem=recv_sem, device_id=device, device_id_type=MESH
        ).start()

    def await_bytes(ref, sem):
        pltpu.make_async_copy(ref, ref, sem).wait()

    def got(kind, i):
        return recv.at[kind * GROUP + i]

    own_slot, fresh_slot = 1 + 7 * c, 9 - 9 * c

    load_q = pltpu.make_async_copy(fresh_q.at[0], q_raw, load_sem.at[0])
    load_k = pltpu.make_async_copy(fresh_k.at[0], k_raw, load_sem.at[1])
    load_q.start()
    load_k.start()

    peers = [at(dx, 0, core) for dx in (1, 3) for core in (0, 1)]
    peers += [at(0, dy, core) for dy in (1, 2, 3) for core in (0, 1)]
    peers += [at(0, 0, sib), (p, 1 - t, g), (p, 1 - t, 1 - g), (p, t, 1 - g)]
    barrier = pltpu.get_barrier_semaphore()
    for peer in peers:
        pl.semaphore_signal(barrier, inc=1, device_id=peer, device_id_type=MESH)

    def local_stale(i, start):
        columns = head_columns(GROUP * c + i)
        copies = (
            pltpu.make_async_copy(stale_k.at[0, :, columns], kb.at[i, block_rows(own_slot), :], local_sem.at[i, 0]),
            pltpu.make_async_copy(stale_v.at[0, :, columns], vb.at[i, block_rows(own_slot), :], local_sem.at[i, 1]),
            pltpu.make_async_copy(fresh_v.at[0, :, columns], vb.at[i, block_rows(fresh_slot), :], local_sem.at[i, 2]),
        )
        for copy in copies:
            copy.start() if start else copy.wait()

    own_heads = pl.ds(GROUP * c, GROUP)
    local_rotated = (
        pltpu.make_async_copy(k_rot.at[own_heads], kb.at[:, block_rows(fresh_slot), :], load_sem.at[8]),
        pltpu.make_async_copy(q_rot.at[own_heads], qb.at[:, block_rows(c), :], load_sem.at[9]),
    )

    def send_own(i, *cores):
        for core in cores or (0, 1):
            columns = head_columns(GROUP * core + i)
            for tensor, (source, buf) in enumerate(((stale_k, kb), (stale_v, vb))):
                for way, (dx, slot, kind) in enumerate(((1, 2, 2 * tensor), (3, 4, 2 * tensor + 1))):
                    send(
                        source.at[0, :, columns],
                        buf.at[i, block_rows(slot + c), :],
                        kv_sem.at[i, core * 4 + tensor * 2 + way],
                        got(kind, i),
                        at(dx, 0, core),
                    )

    def send_sibling_stale(i):
        columns = head_columns(GROUP * sib + i)
        device = at(0, 0, sib)
        send(stale_k.at[0, :, columns], kb.at[i, block_rows(own_slot), :], sib_sem.at[i, 0], got(SIB_K, i), device)
        send(stale_v.at[0, :, columns], vb.at[i, block_rows(own_slot), :], sib_sem.at[i, 1], got(SIB_V, i), device)
        send(fresh_v.at[0, :, columns], vb.at[i, block_rows(fresh_slot), :], sib_sem.at[i, 2], got(SIB_FV, i), device)

    def send_rotated():
        heads = pl.ds(GROUP * sib, GROUP)
        device = at(0, 0, sib)
        send(q_rot.at[heads], qb.at[:, block_rows(c), :], sib_sem.at[0, 3], got(SIB_Q, 0), device)
        send(k_rot.at[heads], kb.at[:, block_rows(fresh_slot), :], sib_sem.at[0, 4], got(SIB_FK, 0), device)

    def send_queries(i):
        for core in (0, 1):
            for way, (dy, block, kind) in enumerate(((1, 6, Q_LEFT), (3, 2, Q_RIGHT))):
                send(
                    q_rot.at[GROUP * core + i],
                    qb.at[i, block_rows(block + c), :],
                    q_sem.at[i, core * 2 + way],
                    got(kind, i),
                    at(0, dy, core),
                )

    def forward_queries(i):
        await_bytes(qb.at[i, block_rows(6, 2), :], got(Q_LEFT, i))
        send(qb.at[i, block_rows(6), :], qb.at[i, block_rows(4), :], far_sem.at[i, 2], got(Q_FAR, i), at(0, 1, c))
        await_bytes(qb.at[i, block_rows(2, 2), :], got(Q_RIGHT, i))
        send(qb.at[i, block_rows(3), :], qb.at[i, block_rows(5), :], far_sem.at[i, 3], got(Q_FAR, i), at(0, 3, c))

    def forward_keys(i):
        await_bytes(kb.at[i, block_rows(2, 2), :], got(K_LEFT, i))
        send(
            kb.at[i, block_rows(2, 2), :], kb.at[i, block_rows(6, 2), :], far_sem.at[i, 0], got(K_FAR, i), at(1, 0, c)
        )
        await_bytes(vb.at[i, block_rows(4, 2), :], got(V_RIGHT, i))
        send(
            vb.at[i, block_rows(4, 2), :], vb.at[i, block_rows(6, 2), :], far_sem.at[i, 1], got(V_FAR, i), at(3, 0, c)
        )

    def arrived(i):
        local_stale(i, False)
        other = 8 - 7 * c
        other_fresh = 9 * c
        await_bytes(kb.at[i, block_rows(other), :], got(SIB_K, i))
        await_bytes(vb.at[i, block_rows(other), :], got(SIB_V, i))
        await_bytes(vb.at[i, block_rows(other_fresh), :], got(SIB_FV, i))

        @pl.when(i == 0)
        def _():
            for copy in local_rotated:
                copy.wait()
            await_bytes(kb.at[:, block_rows(other_fresh), :], got(SIB_FK, 0))
            await_bytes(qb.at[:, block_rows(sib), :], got(SIB_Q, 0))

        await_bytes(kb.at[i, block_rows(4, 2), :], got(K_RIGHT, i))
        await_bytes(vb.at[i, block_rows(2, 2), :], got(V_LEFT, i))
        await_bytes(kb.at[i, block_rows(6, 2), :], got(K_FAR, i))
        await_bytes(vb.at[i, block_rows(6, 2), :], got(V_FAR, i))
        await_bytes(qb.at[i, block_rows(4, 2), :], got(Q_FAR, i))

    res_columns = residual.shape[2] // 2
    mine = pl.ds(pl.multiple_of(g * res_columns, HEAD_DIM), res_columns)
    partner = pl.ds(pl.multiple_of((1 - g) * res_columns, HEAD_DIM), res_columns)

    where_at = positions[...].astype(F32)
    row_of = lax.broadcasted_iota(jnp.int32, (8, ROWS), 0)
    places = jnp.where(
        row_of == 0, where_at[0:1], jnp.where(row_of == 1, where_at[1:2], jnp.where(row_of == 2, where_at[2:3], 0.0))
    )
    angles = lax.dot_general(
        places, freqs[...], (((0,), (0,)), ((), ())), precision=lax.Precision.HIGHEST, preferred_element_type=F32
    )
    cosines[...] = jnp.cos(angles)
    sines[...] = jnp.sin(angles)
    row_ids = lax.broadcasted_iota(jnp.int32, (HEAD_DIM, HEAD_DIM), 0)
    col_ids = lax.broadcasted_iota(jnp.int32, (HEAD_DIM, HEAD_DIM), 1)
    swap = jnp.where(
        (row_ids % 2 == 1) & (col_ids == row_ids - 1),
        -1.0,
        jnp.where((row_ids % 2 == 0) & (col_ids == row_ids + 1), 1.0, 0.0),
    ).astype(BF)

    def rotated(raw, head):
        values = raw[:, head_columns(head)]
        turned = jnp.dot(values, swap, preferred_element_type=F32)
        return (values.astype(F32) * cosines[...] + turned * sines[...]).astype(BF)

    load_q.wait()
    load_k.wait()

    @pl.loop(0, GROUP)
    def _(i):
        for core in (0, 1):
            head = GROUP * core + i
            q_rot[head] = rotated(q_raw, head)
            k_rot[head] = rotated(k_raw, head)

    pl.semaphore_wait(barrier, len(peers))

    send_own(0)
    send_queries(0)
    send_rotated()
    send_sibling_stale(0)
    local_stale(0, True)
    for copy in local_rotated:
        copy.start()
    send_own(1, 0)
    send_queries(1)

    @pl.loop(1, GROUP)
    def _(i):
        send_sibling_stale(i)
        local_stale(i, True)

    send(residual.at[0, :, partner], res_other, res_sem.at[0], res_sem.at[1], (p, t, 1 - g))
    width = 2 * HALF
    starts = (
        (2 * (1 - t) + g) * width,
        (2 * (1 - t) + 1 - g) * width + HALF,
        (2 * t + g) * width,
        (2 * t + g) * width + HALF,
    )
    loads = [
        pltpu.make_async_copy(
            weight.at[:, pl.ds(pl.multiple_of(start, HEAD_DIM), HALF)], w_tiles.at[k], load_sem.at[2 + k]
        )
        for k, start in enumerate(starts)
    ]
    loads.append(pltpu.make_async_copy(residual.at[0, :, mine], res_own, load_sem.at[6]))
    loads.append(
        pltpu.make_async_copy(
            gate_table.at[:, pl.ds(pl.multiple_of((2 * t + g) * width, HEAD_DIM), width)], gate_rows, load_sem.at[7]
        )
    )
    for copy in loads:
        copy.start()

    def pieces(chip):
        if chip:
            return [(0, 2 * ROWS, ROWS)]
        return [(0, ROWS, 2 * ROWS), (ROWS, 2 * ROWS, 0)]

    def score(i, chip, scores):
        for first, last, keys in pieces(chip):
            scores[first:last, :] = lax.dot_general(
                qb[i, 2 * chip * ROWS + first : 2 * chip * ROWS + last, :],
                kb[i, keys : keys + KEYS, :],
                (((1,), (1,)), ((), ())),
                preferred_element_type=F32,
            )

    def soften(i, chip, scores, weights):
        for half in (0, 1):
            rows = slice(half * ROWS, (half + 1) * ROWS)
            top = jnp.max(scores[rows, :], axis=1, keepdims=True) * SCORE_SCALE
            expo = jnp.exp2(scores[rows, :] * SCORE_SCALE - top)
            total = jnp.sum(expo, axis=1, keepdims=True)
            weights[rows, :] = expo.astype(BF)
            notes = jnp.zeros((NOTE, HEAD_DIM), F32)
            note_row = lax.broadcasted_iota(jnp.int32, (NOTE, HEAD_DIM), 0)
            for part, (first, last) in enumerate(((0, HEAD_DIM), (HEAD_DIM, ROWS))):
                for k, (column, count) in enumerate(((top, 3), (total, 2))):
                    rest = jnp.sum(jnp.where(same_lane(last - first), column[first:last], 0.0), axis=0, keepdims=True)
                    for piece in range(count):
                        line = rest.astype(BF).astype(F32)
                        rest = rest - line
                        notes = jnp.where(note_row == 8 * part + 3 * k + piece, line, notes)
            o_send[i, 2 * chip + half, ROWS:, :] = notes.astype(BF)

    def weigh(i, chip, weights):
        for first, last, keys in pieces(chip):
            summed = jnp.dot(
                weights[first:last, :], vb[i, keys : keys + KEYS, :], preferred_element_type=F32
            ).astype(BF)
            for row in range(first, last, ROWS):
                o_send[i, 2 * chip + row // ROWS, 0:ROWS, :] = summed[row - first : row - first + ROWS]

    def send_back(i, b):
        block, core = b // 2, b % 2

        def away():
            place = (RING - block) % RING
            send(
                o_send.at[i, b],
                o_recv.at[GROUP * c + i, place],
                o_sem.at[i, b],
                o_recv_sem.at[GROUP * c + i, place],
                at(0, block, core),
            )

        if block:
            away()
        else:
            pl.when(core != c)(away)

            @pl.when(core == c)
            def _():
                pltpu.make_async_copy(
                    o_send.at[i, b], o_recv.at[GROUP * c + i, 0], o_recv_sem.at[GROUP * c + i, 0]
                ).start()

    def merge(head):
        for j in range(RING):
            await_bytes(o_recv.at[head, j], o_recv_sem.at[head, j])
        notes = [o_recv[head, j, ROWS:, :].astype(F32) for j in range(RING)]
        for part, (first, last) in enumerate(((0, HEAD_DIM), (HEAD_DIM, ROWS))):
            lines = [[n[8 * part + k : 8 * part + k + 1] for k in range(5)] for n in notes]
            tops = [line[0] + line[1] + line[2] for line in lines]
            totals = [line[3] + line[4] for line in lines]
            top = jnp.maximum(jnp.maximum(tops[0], tops[1]), jnp.maximum(tops[2], tops[3]))
            fades = [jnp.exp2(one - top) for one in tops]
            whole = fades[0] * totals[0] + fades[1] * totals[1] + fades[2] * totals[2] + fades[3] * totals[3]
            result = jnp.zeros((last - first, HEAD_DIM), F32)
            for j in range(RING):
                column = jnp.sum(
                    jnp.where(same_lane(last - first), fades[j] / whole, 0.0), axis=1, keepdims=True
                )
                result = result + o_recv[head, j, first:last, :].astype(F32) * column
            attn[head, first:last, :] = result.astype(BF)
        send(attn.at[head], attn_other.at[head], guide_send.at[head], guide_recv.at[head], (p, t, 1 - g))

    forward_queries(0)
    send_queries(2)
    forward_keys(0)
    send_own(1, 1)
    send_own(2)

    @pl.loop(0, GROUP)
    def _(i):
        @pl.when(i < GROUP - 1)
        def _():
            forward_queries(i + 1)
            forward_keys(i + 1)

        @pl.when(i < GROUP - 3)
        def _():
            send_queries(i + 3)
            send_own(i + 3)

        arrived(i)

        order = (2, 3, 1, 0)
        scores = (scores_a, scores_b)
        weights = (weights_a, weights_b)
        for n in range(len(order) + 2):
            if n >= 2:
                weigh(i, order[n - 2], weights[n % 2])
            if n < len(order):
                score(i, order[n], scores[n % 2])
            if 1 <= n <= len(order):
                soften(i, order[n - 1], scores[(n - 1) % 2], weights[(n - 1) % 2])
            if n >= 2:
                send_back(i, 2 * order[n - 2])
                send_back(i, 2 * order[n - 2] + 1)

        @pl.when(i > 0)
        def _():
            merge(i - 1)
            merge(GROUP + i - 1)

    @pl.loop(0, GROUP)
    def _(i):
        for k in range(8):
            await_bytes(kb.at[i, block_rows(0), :], kv_sem.at[i, k])
        for k in range(4):
            await_bytes(q_rot.at[i], q_sem.at[i, k])
        await_bytes(kb.at[i, block_rows(2, 2), :], far_sem.at[i, 0])
        await_bytes(vb.at[i, block_rows(4, 2), :], far_sem.at[i, 1])
        await_bytes(qb.at[i, block_rows(6), :], far_sem.at[i, 2])
        await_bytes(qb.at[i, block_rows(3), :], far_sem.at[i, 3])
        for k in range(3):
            await_bytes(q_rot.at[i], sib_sem.at[i, k])

    for k in (3, 4):
        await_bytes(q_rot.at[0:GROUP], sib_sem.at[0, k])
    for copy in loads:
        copy.wait()
    await_bytes(res_other, res_sem.at[0])
    await_bytes(res_other, res_sem.at[1])
    own_share = (GUIDE_SCALE - (2 * GUIDE_SCALE - 1) * g).astype(F32)
    other_share = (1.0 - GUIDE_SCALE + (2 * GUIDE_SCALE - 1) * g).astype(F32)
    base[...] = own_share * res_own[...].astype(F32) + other_share * res_other[...].astype(F32)
    steps = lax.broadcasted_iota(jnp.int32, gate_rows.shape, 0)
    gate = jnp.sum(jnp.where(steps == timestep[0], gate_rows[...], 0.0), axis=0, keepdims=True)

    merge(GROUP - 1)
    merge(2 * GROUP - 1)

    def combine(head):
        await_bytes(attn_other.at[head], guide_recv.at[head])
        both = own_share * attn[head].astype(F32) + other_share * attn_other[head].astype(F32)
        combined[:, head_columns(head)] = both.astype(BF)

    late = (slice((GROUP - 1) * HEAD_DIM, GROUP * HEAD_DIM), slice((HEADS - 1) * HEAD_DIM, HEADS * HEAD_DIM))
    early = (slice(0, (GROUP - 1) * HEAD_DIM), slice(GROUP * HEAD_DIM, (HEADS - 1) * HEAD_DIM))

    def project(k, spans):
        first, second = (
            jnp.dot(combined[:, span], w_tiles[k, span, :], preferred_element_type=F32) for span in spans
        )
        return first + second

    @pl.loop(0, GROUP - 1)
    def _(i):
        combine(i)
        combine(GROUP + i)

    @pl.loop(0, 4)
    def _(k):
        part[k] = project(k, early)

    combine(GROUP - 1)
    combine(HEADS - 1)
    neighbours = ((p, 1 - t, g), (p, 1 - t, 1 - g))
    for k in (0, 1):
        part_send[k] = (part[k] + project(k, late)).astype(BF)
        send(part_send.at[k], part_recv.at[k], part_send_sem.at[k], part_recv_sem.at[k], neighbours[k])
    for k in (2, 3):
        part[k] = part[k] + project(k, late)

    @pl.loop(0, GROUP)
    def _(i):
        for b in range(2):
            @pl.when(b != c)
            def _():
                await_bytes(o_send.at[i, b], o_sem.at[i, b])

        for b in range(2, 8):
            await_bytes(o_send.at[i, b], o_sem.at[i, b])
        await_bytes(attn.at[i], guide_send.at[i])
        await_bytes(attn.at[GROUP + i], guide_send.at[GROUP + i])

    for k in (0, 1):
        columns = slice(k * HALF, (k + 1) * HALF)
        await_bytes(part_recv.at[k], part_recv_sem.at[k])
        proj = part[2 + k] + part_recv[k].astype(F32)
        out[:, columns] = (base[:, columns] + gate[:, columns] * proj).astype(BF)
    for k in (0, 1):
        await_bytes(part_send.at[k], part_send_sem.at[k])


def per_device(
    fresh_q, fresh_k, fresh_v, stale_k, stale_v, positions, residual, out_weight, gate_table, timestep
):
    width = 2 * HALF
    steps = gate_table.shape[0]
    in_hbm = pl.BlockSpec(memory_space=pl.ANY)
    in_vmem = pl.BlockSpec(memory_space=pltpu.VMEM)
    dma = pltpu.SemaphoreType.DMA
    return pl.pallas_call(
        kernel,
        out_shape=jax.ShapeDtypeStruct((ROWS, width), BF),
        in_specs=[in_hbm] * 8 + [in_vmem, in_vmem, pl.BlockSpec(memory_space=pltpu.SMEM)],
        out_specs=in_vmem,
        scratch_shapes=[
            pltpu.VMEM((GROUP, 10 * ROWS, HEAD_DIM), BF),
            pltpu.VMEM((GROUP, 10 * ROWS, HEAD_DIM), BF),
            pltpu.VMEM((GROUP, 8 * ROWS, HEAD_DIM), BF),
            pltpu.VMEM((2 * ROWS, KEYS), F32),
            pltpu.VMEM((2 * ROWS, KEYS), F32),
            pltpu.VMEM((2 * ROWS, KEYS), BF),
            pltpu.VMEM((2 * ROWS, KEYS), BF),
            pltpu.VMEM((ROWS, width), BF),
            pltpu.VMEM((ROWS, width), BF),
            pltpu.VMEM((HEADS, ROWS, HEAD_DIM), BF),
            pltpu.VMEM((HEADS, ROWS, HEAD_DIM), BF),
            pltpu.VMEM((GROUP, 8, ROWS + NOTE, HEAD_DIM), BF),
            pltpu.VMEM((HEADS, RING, ROWS + NOTE, HEAD_DIM), BF),
            pltpu.VMEM((HEADS, ROWS, HEAD_DIM), BF),
            pltpu.VMEM((HEADS, ROWS, HEAD_DIM), BF),
            pltpu.VMEM((ROWS, width), BF),
            pltpu.VMEM((4, width, HALF), BF),
            pltpu.VMEM((2, ROWS, HALF), BF),
            pltpu.VMEM((2, ROWS, HALF), BF),
            pltpu.VMEM((4, ROWS, HALF), F32),
            pltpu.VMEM((ROWS, width), F32),
            pltpu.VMEM((ROWS, width), BF),
            pltpu.VMEM((ROWS, width), BF),
            pltpu.VMEM((steps, width), F32),
            pltpu.VMEM((ROWS, HEAD_DIM), F32),
            pltpu.VMEM((ROWS, HEAD_DIM), F32),
            dma((KINDS * GROUP,)),
            dma((HEADS, RING)),
            dma((GROUP, 8)),
            dma((GROUP, 4)),
            dma((GROUP, 4)),
            dma((GROUP, 5)),
            dma((GROUP, 5)),
            dma((GROUP, 8)),
            dma((HEADS,)),
            dma((HEADS,)),
            dma((2,)),
            dma((2,)),
            dma((2,)),
            dma((10,)),
        ],
        compiler_params=pltpu.CompilerParams(
            collective_id=0, has_side_effects=True, vmem_limit_bytes=56 * 1024 * 1024
        ),
        cost_estimate=pl.CostEstimate(flops=8_000_000_000, bytes_accessed=12_000_000, transcendentals=12_000_000),
    )(
        fresh_q, fresh_k, fresh_v, stale_k, stale_v, residual, out_weight, gate_table,
        jnp.asarray(frequencies()), positions, timestep,
    )


def solution(mesh):
    in_specs = (
        P("guide", "patch", "tensor"),
        P("guide", "patch", "tensor"),
        P("guide", "patch", "tensor"),
        P("guide", "patch", "tensor"),
        P("guide", "patch", "tensor"),
        P(None, "patch"),
        P("guide", "patch", "tensor"),
        P("tensor", None),
        P(),
        P(),
    )
    out_specs = P("patch", ("tensor", "guide"))
    return jax.shard_map(per_device, mesh=mesh, in_specs=in_specs, out_specs=out_specs, check_vma=False)
```

```python
import functools
import math

import jax
import jax.numpy as jnp
import numpy as np
from jax import lax
from jax.experimental import pallas as pl
from jax.experimental.pallas import tpu as pltpu
from jax.sharding import PartitionSpec as P

MESH = pl.DeviceIdType.MESH
BF = jnp.bfloat16
F32 = jnp.float32
HEAD_DIM = 128
GUIDE_SCALE = 5.0
RING = 4
ROWS = 192
GROUP = 5
HEADS = 10
KEYS = 8 * ROWS
NOTE = 16
EARLY = 3
LATE = GROUP - EARLY
HALF = 640
SCORE_SCALE = math.log2(math.e) / math.sqrt(HEAD_DIM)

(K_LEFT, K_RIGHT, V_LEFT, V_RIGHT, K_FAR, V_FAR, Q_LEFT, Q_RIGHT, Q_FAR, SIB_K, SIB_V, SIB_FK, SIB_FV, SIB_Q) = range(14)
KINDS = 14


def frequencies():
    half_dim = HEAD_DIM // 2
    side_pairs = HEAD_DIM // 6
    frame_pairs = half_dim - 2 * side_pairs
    table = np.zeros((8, HEAD_DIM), np.float32)
    for pair in range(half_dim):
        if pair < frame_pairs:
            section, local, size = 0, pair, frame_pairs
        elif pair < frame_pairs + side_pairs:
            section, local, size = 1, pair - frame_pairs, side_pairs
        else:
            section, local, size = 2, pair - frame_pairs - side_pairs, side_pairs
        table[section, 2 * pair : 2 * pair + 2] = 10000.0 ** (-local / size)
    return table


def block_rows(index, count=1):
    return pl.ds(pl.multiple_of(index * ROWS, ROWS), count * ROWS)


def head_columns(head):
    return pl.ds(pl.multiple_of(head * HEAD_DIM, HEAD_DIM), HEAD_DIM)


def same_lane(rows):
    shape = (rows, HEAD_DIM)
    return lax.broadcasted_iota(jnp.int32, shape, 0) == lax.broadcasted_iota(jnp.int32, shape, 1)


def kernel(
    fresh_q, fresh_k, fresh_v, stale_k, stale_v, residual, weight, gate_table, freqs, positions, timestep,
    out,
    kb, vb, qb, scores_a, scores_b, weights_a, weights_b, q_raw, k_raw, q_rot, k_rot, o_send, o_recv, attn, attn_other,
    combined, combined_far, w_tiles, w_far, part_send, part_recv,
    part, base, res_own, res_other, gate_rows, cosines, sines,
    recv, o_recv_sem, kv_sem, q_sem, far_sem, sib_sem, local_sem, o_sem, guide_send, guide_recv, part_send_sem,
    part_recv_sem, res_sem, load_sem, w_sem, combined_send, combined_recv,
):
    p, t, g = lax.axis_index("patch"), lax.axis_index("tensor"), lax.axis_index("guide")
    x, y, c = p // (2 * RING), (p // 2) % RING, p % 2
    sib = 1 - c

    def at(dx, dy, core):
        return (((x + dx) % RING * RING + (y + dy) % RING) * 2 + core, t, g)

    def send(src, dst, send_sem, recv_sem, device):
        pltpu.make_async_remote_copy(
            src_ref=src, dst_ref=dst, send_sem=send_sem, recv_sem=recv_sem, device_id=device, device_id_type=MESH
        ).start()

    def await_bytes(ref, sem):
        pltpu.make_async_copy(ref, ref, sem).wait()

    def got(kind, i):
        return recv.at[kind * GROUP + i]

    own_slot, fresh_slot = 1 + 7 * c, 9 - 9 * c

    load_q = pltpu.make_async_copy(fresh_q.at[0], q_raw, load_sem.at[0])
    load_k = pltpu.make_async_copy(fresh_k.at[0], k_raw, load_sem.at[1])
    load_q.start()
    load_k.start()

    peers = [at(dx, 0, core) for dx in (1, 3) for core in (0, 1)]
    peers += [at(0, dy, core) for dy in (1, 2, 3) for core in (0, 1)]
    peers += [at(0, 0, sib), (p, 1 - t, g), (p, 1 - t, 1 - g), (p, t, 1 - g)]
    barrier = pltpu.get_barrier_semaphore()
    for peer in peers:
        pl.semaphore_signal(barrier, inc=1, device_id=peer, device_id_type=MESH)

    def local_stale(i, start):
        columns = head_columns(GROUP * c + i)
        copies = (
            pltpu.make_async_copy(stale_k.at[0, :, columns], kb.at[i, block_rows(own_slot), :], local_sem.at[i, 0]),
            pltpu.make_async_copy(stale_v.at[0, :, columns], vb.at[i, block_rows(own_slot), :], local_sem.at[i, 1]),
            pltpu.make_async_copy(fresh_v.at[0, :, columns], vb.at[i, block_rows(fresh_slot), :], local_sem.at[i, 2]),
        )
        for copy in copies:
            copy.start() if start else copy.wait()

    own_heads = pl.ds(GROUP * c, GROUP)
    local_rotated = (
        pltpu.make_async_copy(k_rot.at[own_heads], kb.at[:, block_rows(fresh_slot), :], load_sem.at[8]),
        pltpu.make_async_copy(q_rot.at[own_heads], qb.at[:, block_rows(c), :], load_sem.at[9]),
    )

    def send_own(i, *cores):
        for core in cores or (0, 1):
            columns = head_columns(GROUP * core + i)
            for tensor, (source, buf) in enumerate(((stale_k, kb), (stale_v, vb))):
                for way, (dx, slot, kind) in enumerate(((1, 2, 2 * tensor), (3, 4, 2 * tensor + 1))):
                    send(
                        source.at[0, :, columns],
                        buf.at[i, block_rows(slot + c), :],
                        kv_sem.at[i, core * 4 + tensor * 2 + way],
                        got(kind, i),
                        at(dx, 0, core),
                    )

    def send_sibling_stale(i):
        columns = head_columns(GROUP * sib + i)
        device = at(0, 0, sib)
        send(stale_k.at[0, :, columns], kb.at[i, block_rows(own_slot), :], sib_sem.at[i, 0], got(SIB_K, i), device)
        send(stale_v.at[0, :, columns], vb.at[i, block_rows(own_slot), :], sib_sem.at[i, 1], got(SIB_V, i), device)
        send(fresh_v.at[0, :, columns], vb.at[i, block_rows(fresh_slot), :], sib_sem.at[i, 2], got(SIB_FV, i), device)

    def send_rotated():
        heads = pl.ds(GROUP * sib, GROUP)
        device = at(0, 0, sib)
        send(q_rot.at[heads], qb.at[:, block_rows(c), :], sib_sem.at[0, 3], got(SIB_Q, 0), device)
        send(k_rot.at[heads], kb.at[:, block_rows(fresh_slot), :], sib_sem.at[0, 4], got(SIB_FK, 0), device)

    def send_queries(i):
        for core in (0, 1):
            for way, (dy, block, kind) in enumerate(((1, 6, Q_LEFT), (3, 2, Q_RIGHT))):
                send(
                    q_rot.at[GROUP * core + i],
                    qb.at[i, block_rows(block + c), :],
                    q_sem.at[i, core * 2 + way],
                    got(kind, i),
                    at(0, dy, core),
                )

    def forward_queries(i):
        await_bytes(qb.at[i, block_rows(6, 2), :], got(Q_LEFT, i))
        send(qb.at[i, block_rows(6), :], qb.at[i, block_rows(4), :], far_sem.at[i, 2], got(Q_FAR, i), at(0, 1, c))
        await_bytes(qb.at[i, block_rows(2, 2), :], got(Q_RIGHT, i))
        send(qb.at[i, block_rows(3), :], qb.at[i, block_rows(5), :], far_sem.at[i, 3], got(Q_FAR, i), at(0, 3, c))

    def forward_keys(i):
        await_bytes(kb.at[i, block_rows(2, 2), :], got(K_LEFT, i))
        send(
            kb.at[i, block_rows(2, 2), :], kb.at[i, block_rows(6, 2), :], far_sem.at[i, 0], got(K_FAR, i), at(1, 0, c)
        )
        await_bytes(vb.at[i, block_rows(4, 2), :], got(V_RIGHT, i))
        send(
            vb.at[i, block_rows(4, 2), :], vb.at[i, block_rows(6, 2), :], far_sem.at[i, 1], got(V_FAR, i), at(3, 0, c)
        )

    def arrived(i):
        local_stale(i, False)
        other = 8 - 7 * c
        other_fresh = 9 * c
        await_bytes(kb.at[i, block_rows(other), :], got(SIB_K, i))
        await_bytes(vb.at[i, block_rows(other), :], got(SIB_V, i))
        await_bytes(vb.at[i, block_rows(other_fresh), :], got(SIB_FV, i))

        @pl.when(i == 0)
        def _():
            for copy in local_rotated:
                copy.wait()
            await_bytes(kb.at[:, block_rows(other_fresh), :], got(SIB_FK, 0))
            await_bytes(qb.at[:, block_rows(sib), :], got(SIB_Q, 0))

        await_bytes(kb.at[i, block_rows(4, 2), :], got(K_RIGHT, i))
        await_bytes(vb.at[i, block_rows(2, 2), :], got(V_LEFT, i))
        await_bytes(kb.at[i, block_rows(6, 2), :], got(K_FAR, i))
        await_bytes(vb.at[i, block_rows(6, 2), :], got(V_FAR, i))
        await_bytes(qb.at[i, block_rows(4, 2), :], got(Q_FAR, i))

    res_columns = residual.shape[2] // 2
    mine = pl.ds(pl.multiple_of(g * res_columns, HEAD_DIM), res_columns)
    partner = pl.ds(pl.multiple_of((1 - g) * res_columns, HEAD_DIM), res_columns)

    where_at = positions[...].astype(F32)
    row_of = lax.broadcasted_iota(jnp.int32, (8, ROWS), 0)
    places = jnp.where(
        row_of == 0, where_at[0:1], jnp.where(row_of == 1, where_at[1:2], jnp.where(row_of == 2, where_at[2:3], 0.0))
    )
    angles = lax.dot_general(
        places, freqs[...], (((0,), (0,)), ((), ())), precision=lax.Precision.HIGHEST, preferred_element_type=F32
    )
    cosines[...] = jnp.cos(angles)
    sines[...] = jnp.sin(angles)
    row_ids = lax.broadcasted_iota(jnp.int32, (HEAD_DIM, HEAD_DIM), 0)
    col_ids = lax.broadcasted_iota(jnp.int32, (HEAD_DIM, HEAD_DIM), 1)
    swap = jnp.where(
        (row_ids % 2 == 1) & (col_ids == row_ids - 1),
        -1.0,
        jnp.where((row_ids % 2 == 0) & (col_ids == row_ids + 1), 1.0, 0.0),
    ).astype(BF)

    def rotated(raw, head):
        values = raw[:, head_columns(head)]
        turned = jnp.dot(values, swap, preferred_element_type=F32)
        return (values.astype(F32) * cosines[...] + turned * sines[...]).astype(BF)

    load_q.wait()
    load_k.wait()

    @pl.loop(0, GROUP)
    def _(i):
        for core in (0, 1):
            head = GROUP * core + i
            q_rot[head] = rotated(q_raw, head)
            k_rot[head] = rotated(k_raw, head)

    pl.semaphore_wait(barrier, len(peers))

    send_own(0)
    send_queries(0)
    send_rotated()
    send_sibling_stale(0)
    local_stale(0, True)
    for copy in local_rotated:
        copy.start()
    send_own(1, 0)
    send_queries(1)

    @pl.loop(1, GROUP)
    def _(i):
        send_sibling_stale(i)
        local_stale(i, True)

    neighbours = ((p, 1 - t, g), (p, 1 - t, 1 - g))
    late_rows = tuple(slice((group * GROUP + EARLY) * HEAD_DIM, (group + 1) * GROUP * HEAD_DIM) for group in (0, 1))
    early_rows = tuple(slice(group * GROUP * HEAD_DIM, (group * GROUP + EARLY) * HEAD_DIM) for group in (0, 1))
    for k, branch in enumerate((g, 1 - g)):
        theirs = pl.ds(pl.multiple_of((2 * (1 - t) + branch) * 2 * HALF, HEAD_DIM), 2 * HALF)
        send(weight.at[late_rows[k], theirs], w_far.at[k], w_sem.at[k], w_sem.at[2 + k], neighbours[k])
    send(residual.at[0, :, partner], res_other, res_sem.at[0], res_sem.at[1], (p, t, 1 - g))
    width = 2 * HALF
    starts = (
        (2 * (1 - t) + g) * width,
        (2 * (1 - t) + 1 - g) * width + HALF,
        (2 * t + g) * width,
        (2 * t + g) * width + HALF,
    )
    loads = [
        pltpu.make_async_copy(
            weight.at[:, pl.ds(pl.multiple_of(start, HEAD_DIM), HALF)], w_tiles.at[k], load_sem.at[2 + k]
        )
        for k, start in enumerate(starts)
    ]
    loads.append(pltpu.make_async_copy(residual.at[0, :, mine], res_own, load_sem.at[6]))
    loads.append(
        pltpu.make_async_copy(
            gate_table.at[:, pl.ds(pl.multiple_of((2 * t + g) * width, HEAD_DIM), width)], gate_rows, load_sem.at[7]
        )
    )
    for copy in loads:
        copy.start()

    def pieces(chip):
        if chip:
            return [(0, 2 * ROWS, ROWS)]
        return [(0, ROWS, 2 * ROWS), (ROWS, 2 * ROWS, 0)]

    def score(i, chip, scores):
        for first, last, keys in pieces(chip):
            scores[first:last, :] = lax.dot_general(
                qb[i, 2 * chip * ROWS + first : 2 * chip * ROWS + last, :],
                kb[i, keys : keys + KEYS, :],
                (((1,), (1,)), ((), ())),
                preferred_element_type=F32,
            )

    def soften(i, chip, scores, weights):
        for half in (0, 1):
            rows = slice(half * ROWS, (half + 1) * ROWS)
            top = jnp.max(scores[rows, :], axis=1, keepdims=True) * SCORE_SCALE
            expo = jnp.exp2(scores[rows, :] * SCORE_SCALE - top)
            total = jnp.sum(expo, axis=1, keepdims=True)
            weights[rows, :] = expo.astype(BF)
            notes = jnp.zeros((NOTE, HEAD_DIM), F32)
            note_row = lax.broadcasted_iota(jnp.int32, (NOTE, HEAD_DIM), 0)
            for part, (first, last) in enumerate(((0, HEAD_DIM), (HEAD_DIM, ROWS))):
                for k, (column, count) in enumerate(((top, 3), (total, 2))):
                    rest = jnp.sum(jnp.where(same_lane(last - first), column[first:last], 0.0), axis=0, keepdims=True)
                    for piece in range(count):
                        line = rest.astype(BF).astype(F32)
                        rest = rest - line
                        notes = jnp.where(note_row == 8 * part + 3 * k + piece, line, notes)
            o_send[i, 2 * chip + half, ROWS:, :] = notes.astype(BF)

    def weigh(i, chip, weights):
        for first, last, keys in pieces(chip):
            summed = jnp.dot(
                weights[first:last, :], vb[i, keys : keys + KEYS, :], preferred_element_type=F32
            ).astype(BF)
            for row in range(first, last, ROWS):
                o_send[i, 2 * chip + row // ROWS, 0:ROWS, :] = summed[row - first : row - first + ROWS]

    def send_back(i, b):
        block, core = b // 2, b % 2

        def away():
            place = (RING - block) % RING
            send(
                o_send.at[i, b],
                o_recv.at[GROUP * c + i, place],
                o_sem.at[i, b],
                o_recv_sem.at[GROUP * c + i, place],
                at(0, block, core),
            )

        if block:
            away()
        else:
            pl.when(core != c)(away)

            @pl.when(core == c)
            def _():
                pltpu.make_async_copy(
                    o_send.at[i, b], o_recv.at[GROUP * c + i, 0], o_recv_sem.at[GROUP * c + i, 0]
                ).start()

    def merge(head):
        for j in range(RING):
            await_bytes(o_recv.at[head, j], o_recv_sem.at[head, j])
        notes = [o_recv[head, j, ROWS:, :].astype(F32) for j in range(RING)]
        for part, (first, last) in enumerate(((0, HEAD_DIM), (HEAD_DIM, ROWS))):
            lines = [[n[8 * part + k : 8 * part + k + 1] for k in range(5)] for n in notes]
            tops = [line[0] + line[1] + line[2] for line in lines]
            totals = [line[3] + line[4] for line in lines]
            top = jnp.maximum(jnp.maximum(tops[0], tops[1]), jnp.maximum(tops[2], tops[3]))
            fades = [jnp.exp2(one - top) for one in tops]
            whole = fades[0] * totals[0] + fades[1] * totals[1] + fades[2] * totals[2] + fades[3] * totals[3]
            result = jnp.zeros((last - first, HEAD_DIM), F32)
            for j in range(RING):
                column = jnp.sum(
                    jnp.where(same_lane(last - first), fades[j] / whole, 0.0), axis=1, keepdims=True
                )
                result = result + o_recv[head, j, first:last, :].astype(F32) * column
            attn[head, first:last, :] = result.astype(BF)
        send(attn.at[head], attn_other.at[head], guide_send.at[head], guide_recv.at[head], (p, t, 1 - g))

    own_share = (GUIDE_SCALE - (2 * GUIDE_SCALE - 1) * g).astype(F32)
    other_share = (1.0 - GUIDE_SCALE + (2 * GUIDE_SCALE - 1) * g).astype(F32)

    def combine(head):
        await_bytes(attn_other.at[head], guide_recv.at[head])
        both = own_share * attn[head].astype(F32) + other_share * attn_other[head].astype(F32)
        combined[:, head_columns(head)] = both.astype(BF)

    def project(k, spans):
        first, second = (
            jnp.dot(combined[:, span], w_tiles[k, span, :], preferred_element_type=F32) for span in spans
        )
        return first + second

    forward_queries(0)
    send_queries(2)
    forward_keys(0)
    send_own(1, 1)
    send_own(2)

    @pl.loop(0, GROUP)
    def _(i):
        @pl.when(i < GROUP - 1)
        def _():
            forward_queries(i + 1)
            forward_keys(i + 1)

        @pl.when(i < GROUP - 3)
        def _():
            send_queries(i + 3)
            send_own(i + 3)

        arrived(i)

        order = (2, 3, 1, 0)
        scores = (scores_a, scores_b)
        weights = (weights_a, weights_b)
        for n in range(len(order) + 2):
            if n >= 2:
                weigh(i, order[n - 2], weights[n % 2])
            if n < len(order):
                score(i, order[n], scores[n % 2])
            if 1 <= n <= len(order):
                soften(i, order[n - 1], scores[(n - 1) % 2], weights[(n - 1) % 2])
            if n >= 2:
                send_back(i, 2 * order[n - 2])
                send_back(i, 2 * order[n - 2] + 1)

        @pl.when(i > 0)
        def _():
            merge(i - 1)
            merge(GROUP + i - 1)

        @pl.when(i == EARLY + 1)
        def _():
            for copy in loads:
                copy.wait()
            for head in range(EARLY):
                combine(head)
                combine(GROUP + head)
            for k in (0, 1):
                part_send[k] = project(k, early_rows).astype(BF)
                send(part_send.at[k], part_recv.at[k], part_send_sem.at[k], part_recv_sem.at[k], neighbours[k])

    @pl.loop(0, GROUP)
    def _(i):
        for k in range(8):
            await_bytes(kb.at[i, block_rows(0), :], kv_sem.at[i, k])
        for k in range(4):
            await_bytes(q_rot.at[i], q_sem.at[i, k])
        await_bytes(kb.at[i, block_rows(2, 2), :], far_sem.at[i, 0])
        await_bytes(vb.at[i, block_rows(4, 2), :], far_sem.at[i, 1])
        await_bytes(qb.at[i, block_rows(6), :], far_sem.at[i, 2])
        await_bytes(qb.at[i, block_rows(3), :], far_sem.at[i, 3])
        for k in range(3):
            await_bytes(q_rot.at[i], sib_sem.at[i, k])

    for k in (3, 4):
        await_bytes(q_rot.at[0:GROUP], sib_sem.at[0, k])
    await_bytes(res_other, res_sem.at[0])
    await_bytes(res_other, res_sem.at[1])
    base[...] = own_share * res_own[...].astype(F32) + other_share * res_other[...].astype(F32)
    steps = lax.broadcasted_iota(jnp.int32, gate_rows.shape, 0)
    gate = jnp.sum(jnp.where(steps == timestep[0], gate_rows[...], 0.0), axis=0, keepdims=True)

    def exchange(j):
        for group in (0, 1):
            head = group * GROUP + EARLY + j
            combine(head)
            send(
                combined.at[:, head * HEAD_DIM : (head + 1) * HEAD_DIM],
                combined_far.at[group, :, j * HEAD_DIM : (j + 1) * HEAD_DIM],
                combined_send.at[group, j],
                combined_recv.at[group, j],
                neighbours[group],
            )

    for j in range(LATE - 2):
        exchange(j)
    merge(GROUP - 1)
    merge(2 * GROUP - 1)
    exchange(LATE - 2)

    @pl.loop(2, 4)
    def _(k):
        part[k - 2] = project(k, early_rows)

    exchange(LATE - 1)

    @pl.loop(2, 4)
    def _(k):
        part[k - 2] += project(k, late_rows)

    for k in (0, 1):
        await_bytes(w_far.at[k], w_sem.at[k])
        await_bytes(w_far.at[k], w_sem.at[2 + k])

    @pl.loop(0, GROUP)
    def _(i):
        for b in range(2):
            @pl.when(b != c)
            def _():
                await_bytes(o_send.at[i, b], o_sem.at[i, b])

        for b in range(2, 8):
            await_bytes(o_send.at[i, b], o_sem.at[i, b])
        await_bytes(attn.at[i], guide_send.at[i])
        await_bytes(attn.at[GROUP + i], guide_send.at[GROUP + i])

    for k in (0, 1):
        await_bytes(part_recv.at[k], part_recv_sem.at[k])
    for group in (0, 1):
        for j in range(LATE):
            await_bytes(combined_far.at[group, :, j * HEAD_DIM : (j + 1) * HEAD_DIM], combined_recv.at[group, j])
    for k in (0, 1):
        columns = slice(k * HALF, (k + 1) * HALF)
        proj = part[k] + part_recv[k].astype(F32)
        for group in (0, 1):
            proj = proj + jnp.dot(combined_far[group], w_far[group, :, columns], preferred_element_type=F32)
        out[:, columns] = (base[:, columns] + gate[:, columns] * proj).astype(BF)
    for k in (0, 1):
        await_bytes(part_send.at[k], part_send_sem.at[k])
    for group in (0, 1):
        for j in range(LATE):
            await_bytes(attn.at[0], combined_send.at[group, j])


def per_device(
    fresh_q, fresh_k, fresh_v, stale_k, stale_v, positions, residual, out_weight, gate_table, timestep
):
    width = 2 * HALF
    steps = gate_table.shape[0]
    in_hbm = pl.BlockSpec(memory_space=pl.ANY)
    in_vmem = pl.BlockSpec(memory_space=pltpu.VMEM)
    dma = pltpu.SemaphoreType.DMA
    return pl.pallas_call(
        kernel,
        out_shape=jax.ShapeDtypeStruct((ROWS, width), BF),
        in_specs=[in_hbm] * 8 + [in_vmem, in_vmem, pl.BlockSpec(memory_space=pltpu.SMEM)],
        out_specs=in_vmem,
        scratch_shapes=[
            pltpu.VMEM((GROUP, 10 * ROWS, HEAD_DIM), BF),
            pltpu.VMEM((GROUP, 10 * ROWS, HEAD_DIM), BF),
            pltpu.VMEM((GROUP, 8 * ROWS, HEAD_DIM), BF),
            pltpu.VMEM((2 * ROWS, KEYS), F32),
            pltpu.VMEM((2 * ROWS, KEYS), F32),
            pltpu.VMEM((2 * ROWS, KEYS), BF),
            pltpu.VMEM((2 * ROWS, KEYS), BF),
            pltpu.VMEM((ROWS, width), BF),
            pltpu.VMEM((ROWS, width), BF),
            pltpu.VMEM((HEADS, ROWS, HEAD_DIM), BF),
            pltpu.VMEM((HEADS, ROWS, HEAD_DIM), BF),
            pltpu.VMEM((GROUP, 8, ROWS + NOTE, HEAD_DIM), BF),
            pltpu.VMEM((HEADS, RING, ROWS + NOTE, HEAD_DIM), BF),
            pltpu.VMEM((HEADS, ROWS, HEAD_DIM), BF),
            pltpu.VMEM((HEADS, ROWS, HEAD_DIM), BF),
            pltpu.VMEM((ROWS, width), BF),
            pltpu.VMEM((2, ROWS, LATE * HEAD_DIM), BF),
            pltpu.VMEM((4, width, HALF), BF),
            pltpu.VMEM((2, LATE * HEAD_DIM, width), BF),
            pltpu.VMEM((2, ROWS, HALF), BF),
            pltpu.VMEM((2, ROWS, HALF), BF),
            pltpu.VMEM((2, ROWS, HALF), F32),
            pltpu.VMEM((ROWS, width), F32),
            pltpu.VMEM((ROWS, width), BF),
            pltpu.VMEM((ROWS, width), BF),
            pltpu.VMEM((steps, width), F32),
            pltpu.VMEM((ROWS, HEAD_DIM), F32),
            pltpu.VMEM((ROWS, HEAD_DIM), F32),
            dma((KINDS * GROUP,)),
            dma((HEADS, RING)),
            dma((GROUP, 8)),
            dma((GROUP, 4)),
            dma((GROUP, 4)),
            dma((GROUP, 5)),
            dma((GROUP, 5)),
            dma((GROUP, 8)),
            dma((HEADS,)),
            dma((HEADS,)),
            dma((2,)),
            dma((2,)),
            dma((2,)),
            dma((10,)),
            dma((4,)),
            dma((2, LATE)),
            dma((2, LATE)),
        ],
        compiler_params=pltpu.CompilerParams(
            collective_id=0, has_side_effects=True, vmem_limit_bytes=56 * 1024 * 1024
        ),
        cost_estimate=pl.CostEstimate(flops=8_000_000_000, bytes_accessed=12_000_000, transcendentals=12_000_000),
    )(
        fresh_q, fresh_k, fresh_v, stale_k, stale_v, residual, out_weight, gate_table,
        jnp.asarray(frequencies()), positions, timestep,
    )


def solution(mesh):
    in_specs = (
        P("guide", "patch", "tensor"),
        P("guide", "patch", "tensor"),
        P("guide", "patch", "tensor"),
        P("guide", "patch", "tensor"),
        P("guide", "patch", "tensor"),
        P(None, "patch"),
        P("guide", "patch", "tensor"),
        P("tensor", None),
        P(),
        P(),
    )
    out_specs = P("patch", ("tensor", "guide"))
    return jax.shard_map(per_device, mesh=mesh, in_specs=in_specs, out_specs=out_specs, check_vma=False)
```

```python
import functools
import math

import jax
import jax.numpy as jnp
import numpy as np
from jax import lax
from jax.experimental import pallas as pl
from jax.experimental.pallas import tpu as pltpu
from jax.sharding import PartitionSpec as P

MESH = pl.DeviceIdType.MESH
BF = jnp.bfloat16
F32 = jnp.float32
HEAD_DIM = 128
GUIDE_SCALE = 5.0
RING = 4
ROWS = 192
GROUP = 5
HEADS = 10
KEYS = 8 * ROWS
NOTE = 16
EARLY = 3
LATE = GROUP - EARLY
HALF = 640
SCORE_SCALE = math.log2(math.e) / math.sqrt(HEAD_DIM)

(K_LEFT, K_RIGHT, V_LEFT, V_RIGHT, K_FAR, V_FAR, Q_LEFT, Q_RIGHT, Q_FAR, SIB_K, SIB_V, SIB_FK, SIB_FV, SIB_Q) = range(14)
KINDS = 14


def frequencies():
    half_dim = HEAD_DIM // 2
    side_pairs = HEAD_DIM // 6
    frame_pairs = half_dim - 2 * side_pairs
    table = np.zeros((8, HEAD_DIM), np.float32)
    for pair in range(half_dim):
        if pair < frame_pairs:
            section, local, size = 0, pair, frame_pairs
        elif pair < frame_pairs + side_pairs:
            section, local, size = 1, pair - frame_pairs, side_pairs
        else:
            section, local, size = 2, pair - frame_pairs - side_pairs, side_pairs
        table[section, 2 * pair : 2 * pair + 2] = 10000.0 ** (-local / size)
    return table


def block_rows(index, count=1):
    return pl.ds(pl.multiple_of(index * ROWS, ROWS), count * ROWS)


def head_columns(head):
    return pl.ds(pl.multiple_of(head * HEAD_DIM, HEAD_DIM), HEAD_DIM)


def same_lane(rows):
    shape = (rows, HEAD_DIM)
    return lax.broadcasted_iota(jnp.int32, shape, 0) == lax.broadcasted_iota(jnp.int32, shape, 1)


def kernel(
    fresh_q, fresh_k, fresh_v, stale_k, stale_v, residual, weight, gate_table, freqs, positions, timestep,
    out,
    kb, vb, qb, scores_a, scores_b, weights_a, weights_b, q_raw, k_raw, q_rot, k_rot, o_send, o_recv, attn, attn_other,
    combined, combined_far, w_tiles, w_far, part_send, part_recv,
    part, base, res_own, res_other, gate_rows, cosines, sines,
    recv, o_recv_sem, kv_sem, q_sem, far_sem, sib_sem, local_sem, o_sem, guide_send, guide_recv, part_send_sem,
    part_recv_sem, res_sem, load_sem, w_sem, combined_send, combined_recv,
):
    p, t, g = lax.axis_index("patch"), lax.axis_index("tensor"), lax.axis_index("guide")
    x, y, c = p // (2 * RING), (p // 2) % RING, p % 2
    sib = 1 - c

    def at(dx, dy, core):
        return (((x + dx) % RING * RING + (y + dy) % RING) * 2 + core, t, g)

    def send(src, dst, send_sem, recv_sem, device):
        pltpu.make_async_remote_copy(
            src_ref=src, dst_ref=dst, send_sem=send_sem, recv_sem=recv_sem, device_id=device, device_id_type=MESH
        ).start()

    def await_bytes(ref, sem):
        pltpu.make_async_copy(ref, ref, sem).wait()

    def got(kind, i):
        return recv.at[kind * GROUP + i]

    own_slot, fresh_slot = 1 + 7 * c, 9 - 9 * c

    load_q = pltpu.make_async_copy(fresh_q.at[0], q_raw, load_sem.at[0])
    load_k = pltpu.make_async_copy(fresh_k.at[0], k_raw, load_sem.at[1])
    load_q.start()
    load_k.start()

    peers = [at(dx, 0, core) for dx in (1, 3) for core in (0, 1)]
    peers += [at(0, dy, core) for dy in (1, 2, 3) for core in (0, 1)]
    peers += [at(0, 0, sib), (p, 1 - t, g), (p, 1 - t, 1 - g), (p, t, 1 - g)]
    barrier = pltpu.get_barrier_semaphore()
    for peer in peers:
        pl.semaphore_signal(barrier, inc=1, device_id=peer, device_id_type=MESH)

    def local_stale(i, start):
        columns = head_columns(GROUP * c + i)
        copies = (
            pltpu.make_async_copy(stale_k.at[0, :, columns], kb.at[i, block_rows(own_slot), :], local_sem.at[i, 0]),
            pltpu.make_async_copy(stale_v.at[0, :, columns], vb.at[i, block_rows(own_slot), :], local_sem.at[i, 1]),
            pltpu.make_async_copy(fresh_v.at[0, :, columns], vb.at[i, block_rows(fresh_slot), :], local_sem.at[i, 2]),
        )
        for copy in copies:
            copy.start() if start else copy.wait()

    own_heads = pl.ds(GROUP * c, GROUP)
    local_rotated = (
        pltpu.make_async_copy(k_rot.at[own_heads], kb.at[:, block_rows(fresh_slot), :], load_sem.at[8]),
        pltpu.make_async_copy(q_rot.at[own_heads], qb.at[:, block_rows(c), :], load_sem.at[9]),
    )

    def send_own(i, *cores):
        for core in cores or (0, 1):
            columns = head_columns(GROUP * core + i)
            for tensor, (source, buf) in enumerate(((stale_k, kb), (stale_v, vb))):
                for way, (dx, slot, kind) in enumerate(((1, 2, 2 * tensor), (3, 4, 2 * tensor + 1))):
                    send(
                        source.at[0, :, columns],
                        buf.at[i, block_rows(slot + c), :],
                        kv_sem.at[i, core * 4 + tensor * 2 + way],
                        got(kind, i),
                        at(dx, 0, core),
                    )

    def send_sibling_stale(i):
        columns = head_columns(GROUP * sib + i)
        device = at(0, 0, sib)
        send(stale_k.at[0, :, columns], kb.at[i, block_rows(own_slot), :], sib_sem.at[i, 0], got(SIB_K, i), device)
        send(stale_v.at[0, :, columns], vb.at[i, block_rows(own_slot), :], sib_sem.at[i, 1], got(SIB_V, i), device)
        send(fresh_v.at[0, :, columns], vb.at[i, block_rows(fresh_slot), :], sib_sem.at[i, 2], got(SIB_FV, i), device)

    def send_rotated():
        heads = pl.ds(GROUP * sib, GROUP)
        device = at(0, 0, sib)
        send(q_rot.at[heads], qb.at[:, block_rows(c), :], sib_sem.at[0, 3], got(SIB_Q, 0), device)
        send(k_rot.at[heads], kb.at[:, block_rows(fresh_slot), :], sib_sem.at[0, 4], got(SIB_FK, 0), device)

    def send_queries(i):
        for core in (0, 1):
            for way, (dy, block, kind) in enumerate(((1, 6, Q_LEFT), (3, 2, Q_RIGHT))):
                send(
                    q_rot.at[GROUP * core + i],
                    qb.at[i, block_rows(block + c), :],
                    q_sem.at[i, core * 2 + way],
                    got(kind, i),
                    at(0, dy, core),
                )

    def forward_queries(i):
        await_bytes(qb.at[i, block_rows(6, 2), :], got(Q_LEFT, i))
        send(qb.at[i, block_rows(6), :], qb.at[i, block_rows(4), :], far_sem.at[i, 2], got(Q_FAR, i), at(0, 1, c))
        await_bytes(qb.at[i, block_rows(2, 2), :], got(Q_RIGHT, i))
        send(qb.at[i, block_rows(3), :], qb.at[i, block_rows(5), :], far_sem.at[i, 3], got(Q_FAR, i), at(0, 3, c))

    def forward_keys(i):
        await_bytes(kb.at[i, block_rows(2, 2), :], got(K_LEFT, i))
        send(
            kb.at[i, block_rows(2, 2), :], kb.at[i, block_rows(6, 2), :], far_sem.at[i, 0], got(K_FAR, i), at(1, 0, c)
        )
        await_bytes(vb.at[i, block_rows(4, 2), :], got(V_RIGHT, i))
        send(
            vb.at[i, block_rows(4, 2), :], vb.at[i, block_rows(6, 2), :], far_sem.at[i, 1], got(V_FAR, i), at(3, 0, c)
        )

    def arrived(i):
        local_stale(i, False)
        other = 8 - 7 * c
        other_fresh = 9 * c
        await_bytes(kb.at[i, block_rows(other), :], got(SIB_K, i))
        await_bytes(vb.at[i, block_rows(other), :], got(SIB_V, i))
        await_bytes(vb.at[i, block_rows(other_fresh), :], got(SIB_FV, i))

        @pl.when(i == 0)
        def _():
            for copy in local_rotated:
                copy.wait()
            await_bytes(kb.at[:, block_rows(other_fresh), :], got(SIB_FK, 0))
            await_bytes(qb.at[:, block_rows(sib), :], got(SIB_Q, 0))

        await_bytes(kb.at[i, block_rows(4, 2), :], got(K_RIGHT, i))
        await_bytes(vb.at[i, block_rows(2, 2), :], got(V_LEFT, i))
        await_bytes(kb.at[i, block_rows(6, 2), :], got(K_FAR, i))
        await_bytes(vb.at[i, block_rows(6, 2), :], got(V_FAR, i))
        await_bytes(qb.at[i, block_rows(4, 2), :], got(Q_FAR, i))

    res_columns = residual.shape[2] // 2
    mine = pl.ds(pl.multiple_of(g * res_columns, HEAD_DIM), res_columns)
    partner = pl.ds(pl.multiple_of((1 - g) * res_columns, HEAD_DIM), res_columns)

    where_at = positions[...].astype(F32)
    row_of = lax.broadcasted_iota(jnp.int32, (8, ROWS), 0)
    places = jnp.where(
        row_of == 0, where_at[0:1], jnp.where(row_of == 1, where_at[1:2], jnp.where(row_of == 2, where_at[2:3], 0.0))
    )
    angles = lax.dot_general(
        places, freqs[...], (((0,), (0,)), ((), ())), precision=lax.Precision.HIGHEST, preferred_element_type=F32
    )
    cosines[...] = jnp.cos(angles)
    sines[...] = jnp.sin(angles)
    row_ids = lax.broadcasted_iota(jnp.int32, (HEAD_DIM, HEAD_DIM), 0)
    col_ids = lax.broadcasted_iota(jnp.int32, (HEAD_DIM, HEAD_DIM), 1)
    swap = jnp.where(
        (row_ids % 2 == 1) & (col_ids == row_ids - 1),
        -1.0,
        jnp.where((row_ids % 2 == 0) & (col_ids == row_ids + 1), 1.0, 0.0),
    ).astype(BF)

    def rotated(raw, head):
        values = raw[:, head_columns(head)]
        turned = jnp.dot(values, swap, preferred_element_type=F32)
        return (values.astype(F32) * cosines[...] + turned * sines[...]).astype(BF)

    load_q.wait()
    load_k.wait()

    @pl.loop(0, GROUP)
    def _(i):
        for core in (0, 1):
            head = GROUP * core + i
            q_rot[head] = rotated(q_raw, head)
            k_rot[head] = rotated(k_raw, head)

    pl.semaphore_wait(barrier, len(peers))

    send_own(0)
    send_queries(0)
    send_rotated()
    send_sibling_stale(0)
    local_stale(0, True)
    for copy in local_rotated:
        copy.start()
    send_own(1, 0)
    send_queries(1)

    @pl.loop(1, GROUP)
    def _(i):
        send_sibling_stale(i)
        local_stale(i, True)

    neighbours = ((p, 1 - t, g), (p, 1 - t, 1 - g))
    late_rows = tuple(slice((group * GROUP + EARLY) * HEAD_DIM, (group + 1) * GROUP * HEAD_DIM) for group in (0, 1))
    early_rows = tuple(slice(group * GROUP * HEAD_DIM, (group * GROUP + EARLY) * HEAD_DIM) for group in (0, 1))
    for k, branch in enumerate((g, 1 - g)):
        theirs = pl.ds(pl.multiple_of((2 * (1 - t) + branch) * 2 * HALF, HEAD_DIM), 2 * HALF)
        send(weight.at[late_rows[k], theirs], w_far.at[k], w_sem.at[k], w_sem.at[2 + k], neighbours[k])
    send(residual.at[0, :, partner], res_other, res_sem.at[0], res_sem.at[1], (p, t, 1 - g))
    width = 2 * HALF
    starts = (
        (2 * (1 - t) + g) * width,
        (2 * (1 - t) + 1 - g) * width + HALF,
        (2 * t + g) * width,
        (2 * t + g) * width + HALF,
    )
    loads = [
        pltpu.make_async_copy(
            weight.at[:, pl.ds(pl.multiple_of(start, HEAD_DIM), HALF)], w_tiles.at[k], load_sem.at[2 + k]
        )
        for k, start in enumerate(starts)
    ]
    loads.append(pltpu.make_async_copy(residual.at[0, :, mine], res_own, load_sem.at[6]))
    loads.append(
        pltpu.make_async_copy(
            gate_table.at[:, pl.ds(pl.multiple_of((2 * t + g) * width, HEAD_DIM), width)], gate_rows, load_sem.at[7]
        )
    )

    def pieces(chip):
        if chip:
            return [(0, 2 * ROWS, ROWS)]
        return [(0, ROWS, 2 * ROWS), (ROWS, 2 * ROWS, 0)]

    def score(i, chip, scores):
        for first, last, keys in pieces(chip):
            scores[first:last, :] = lax.dot_general(
                qb[i, 2 * chip * ROWS + first : 2 * chip * ROWS + last, :],
                kb[i, keys : keys + KEYS, :],
                (((1,), (1,)), ((), ())),
                preferred_element_type=F32,
            )

    def soften(i, chip, scores, weights):
        for half in (0, 1):
            rows = slice(half * ROWS, (half + 1) * ROWS)
            top = jnp.max(scores[rows, :], axis=1, keepdims=True) * SCORE_SCALE
            expo = jnp.exp2(scores[rows, :] * SCORE_SCALE - top)
            total = jnp.sum(expo, axis=1, keepdims=True)
            weights[rows, :] = expo.astype(BF)
            notes = jnp.zeros((NOTE, HEAD_DIM), F32)
            note_row = lax.broadcasted_iota(jnp.int32, (NOTE, HEAD_DIM), 0)
            for part, (first, last) in enumerate(((0, HEAD_DIM), (HEAD_DIM, ROWS))):
                for k, (column, count) in enumerate(((top, 3), (total, 2))):
                    rest = jnp.sum(jnp.where(same_lane(last - first), column[first:last], 0.0), axis=0, keepdims=True)
                    for piece in range(count):
                        line = rest.astype(BF).astype(F32)
                        rest = rest - line
                        notes = jnp.where(note_row == 8 * part + 3 * k + piece, line, notes)
            o_send[i, 2 * chip + half, ROWS:, :] = notes.astype(BF)

    def weigh(i, chip, weights):
        for first, last, keys in pieces(chip):
            summed = jnp.dot(
                weights[first:last, :], vb[i, keys : keys + KEYS, :], preferred_element_type=F32
            ).astype(BF)
            for row in range(first, last, ROWS):
                o_send[i, 2 * chip + row // ROWS, 0:ROWS, :] = summed[row - first : row - first + ROWS]

    def send_back(i, b):
        block, core = b // 2, b % 2

        def away():
            place = (RING - block) % RING
            send(
                o_send.at[i, b],
                o_recv.at[GROUP * c + i, place],
                o_sem.at[i, b],
                o_recv_sem.at[GROUP * c + i, place],
                at(0, block, core),
            )

        if block:
            away()
        else:
            pl.when(core != c)(away)

            @pl.when(core == c)
            def _():
                pltpu.make_async_copy(
                    o_send.at[i, b], o_recv.at[GROUP * c + i, 0], o_recv_sem.at[GROUP * c + i, 0]
                ).start()

    def merge(head):
        for j in range(RING):
            await_bytes(o_recv.at[head, j], o_recv_sem.at[head, j])
        notes = [o_recv[head, j, ROWS:, :].astype(F32) for j in range(RING)]
        for part, (first, last) in enumerate(((0, HEAD_DIM), (HEAD_DIM, ROWS))):
            lines = [[n[8 * part + k : 8 * part + k + 1] for k in range(5)] for n in notes]
            tops = [line[0] + line[1] + line[2] for line in lines]
            totals = [line[3] + line[4] for line in lines]
            top = jnp.maximum(jnp.maximum(tops[0], tops[1]), jnp.maximum(tops[2], tops[3]))
            fades = [jnp.exp2(one - top) for one in tops]
            whole = fades[0] * totals[0] + fades[1] * totals[1] + fades[2] * totals[2] + fades[3] * totals[3]
            result = jnp.zeros((last - first, HEAD_DIM), F32)
            for j in range(RING):
                column = jnp.sum(
                    jnp.where(same_lane(last - first), fades[j] / whole, 0.0), axis=1, keepdims=True
                )
                result = result + o_recv[head, j, first:last, :].astype(F32) * column
            attn[head, first:last, :] = result.astype(BF)
        send(attn.at[head], attn_other.at[head], guide_send.at[head], guide_recv.at[head], (p, t, 1 - g))

    own_share = (GUIDE_SCALE - (2 * GUIDE_SCALE - 1) * g).astype(F32)
    other_share = (1.0 - GUIDE_SCALE + (2 * GUIDE_SCALE - 1) * g).astype(F32)

    def combine(head):
        await_bytes(attn_other.at[head], guide_recv.at[head])
        both = own_share * attn[head].astype(F32) + other_share * attn_other[head].astype(F32)
        combined[:, head_columns(head)] = both.astype(BF)

    def project(k, spans):
        first, second = (
            jnp.dot(combined[:, span], w_tiles[k, span, :], preferred_element_type=F32) for span in spans
        )
        return first + second

    forward_queries(0)
    send_queries(2)
    forward_keys(0)
    send_own(1, 1)
    send_own(2)

    @pl.loop(0, GROUP)
    def _(i):
        @pl.when(i < GROUP - 1)
        def _():
            forward_queries(i + 1)
            forward_keys(i + 1)

        @pl.when(i < GROUP - 3)
        def _():
            send_queries(i + 3)
            send_own(i + 3)

        arrived(i)

        order = (2, 3, 1, 0)
        scores = (scores_a, scores_b)
        weights = (weights_a, weights_b)
        for n in range(len(order) + 2):
            if n >= 2:
                weigh(i, order[n - 2], weights[n % 2])
            if n < len(order):
                score(i, order[n], scores[n % 2])
            if 1 <= n <= len(order):
                soften(i, order[n - 1], scores[(n - 1) % 2], weights[(n - 1) % 2])
            if n >= 2:
                send_back(i, 2 * order[n - 2])
                send_back(i, 2 * order[n - 2] + 1)

        @pl.when(i == 0)
        def _():
            for copy in loads:
                copy.start()

        @pl.when(i > 0)
        def _():
            merge(i - 1)
            merge(GROUP + i - 1)

        @pl.when(i == EARLY + 1)
        def _():
            for copy in loads:
                copy.wait()
            for head in range(EARLY):
                combine(head)
                combine(GROUP + head)
            for k in (0, 1):
                part_send[k] = project(k, early_rows).astype(BF)
                send(part_send.at[k], part_recv.at[k], part_send_sem.at[k], part_recv_sem.at[k], neighbours[k])

    @pl.loop(0, GROUP)
    def _(i):
        for k in range(8):
            await_bytes(kb.at[i, block_rows(0), :], kv_sem.at[i, k])
        for k in range(4):
            await_bytes(q_rot.at[i], q_sem.at[i, k])
        await_bytes(kb.at[i, block_rows(2, 2), :], far_sem.at[i, 0])
        await_bytes(vb.at[i, block_rows(4, 2), :], far_sem.at[i, 1])
        await_bytes(qb.at[i, block_rows(6), :], far_sem.at[i, 2])
        await_bytes(qb.at[i, block_rows(3), :], far_sem.at[i, 3])
        for k in range(3):
            await_bytes(q_rot.at[i], sib_sem.at[i, k])

    for k in (3, 4):
        await_bytes(q_rot.at[0:GROUP], sib_sem.at[0, k])
    await_bytes(res_other, res_sem.at[0])
    await_bytes(res_other, res_sem.at[1])
    base[...] = own_share * res_own[...].astype(F32) + other_share * res_other[...].astype(F32)
    steps = lax.broadcasted_iota(jnp.int32, gate_rows.shape, 0)
    gate = jnp.sum(jnp.where(steps == timestep[0], gate_rows[...], 0.0), axis=0, keepdims=True)

    def exchange(j):
        for group in (0, 1):
            head = group * GROUP + EARLY + j
            combine(head)
            send(
                combined.at[:, head * HEAD_DIM : (head + 1) * HEAD_DIM],
                combined_far.at[group, :, j * HEAD_DIM : (j + 1) * HEAD_DIM],
                combined_send.at[group, j],
                combined_recv.at[group, j],
                neighbours[group],
            )

    for j in range(LATE - 2):
        exchange(j)
    merge(GROUP - 1)
    merge(2 * GROUP - 1)
    exchange(LATE - 2)

    @pl.loop(2, 4)
    def _(k):
        part[k - 2] = project(k, early_rows)

    exchange(LATE - 1)

    @pl.loop(2, 4)
    def _(k):
        part[k - 2] += project(k, late_rows)

    for k in (0, 1):
        await_bytes(w_far.at[k], w_sem.at[k])
        await_bytes(w_far.at[k], w_sem.at[2 + k])

    @pl.loop(0, GROUP)
    def _(i):
        for b in range(2):
            @pl.when(b != c)
            def _():
                await_bytes(o_send.at[i, b], o_sem.at[i, b])

        for b in range(2, 8):
            await_bytes(o_send.at[i, b], o_sem.at[i, b])
        await_bytes(attn.at[i], guide_send.at[i])
        await_bytes(attn.at[GROUP + i], guide_send.at[GROUP + i])

    for k in (0, 1):
        await_bytes(part_recv.at[k], part_recv_sem.at[k])
    for group in (0, 1):
        for j in range(LATE):
            await_bytes(combined_far.at[group, :, j * HEAD_DIM : (j + 1) * HEAD_DIM], combined_recv.at[group, j])
    for k in (0, 1):
        columns = slice(k * HALF, (k + 1) * HALF)
        proj = part[k] + part_recv[k].astype(F32)
        for group in (0, 1):
            proj = proj + jnp.dot(combined_far[group], w_far[group, :, columns], preferred_element_type=F32)
        out[:, columns] = (base[:, columns] + gate[:, columns] * proj).astype(BF)
    for k in (0, 1):
        await_bytes(part_send.at[k], part_send_sem.at[k])
    for group in (0, 1):
        for j in range(LATE):
            await_bytes(attn.at[0], combined_send.at[group, j])


def per_device(
    fresh_q, fresh_k, fresh_v, stale_k, stale_v, positions, residual, out_weight, gate_table, timestep
):
    width = 2 * HALF
    steps = gate_table.shape[0]
    in_hbm = pl.BlockSpec(memory_space=pl.ANY)
    in_vmem = pl.BlockSpec(memory_space=pltpu.VMEM)
    dma = pltpu.SemaphoreType.DMA
    return pl.pallas_call(
        kernel,
        out_shape=jax.ShapeDtypeStruct((ROWS, width), BF),
        in_specs=[in_hbm] * 8 + [in_vmem, in_vmem, pl.BlockSpec(memory_space=pltpu.SMEM)],
        out_specs=in_vmem,
        scratch_shapes=[
            pltpu.VMEM((GROUP, 10 * ROWS, HEAD_DIM), BF),
            pltpu.VMEM((GROUP, 10 * ROWS, HEAD_DIM), BF),
            pltpu.VMEM((GROUP, 8 * ROWS, HEAD_DIM), BF),
            pltpu.VMEM((2 * ROWS, KEYS), F32),
            pltpu.VMEM((2 * ROWS, KEYS), F32),
            pltpu.VMEM((2 * ROWS, KEYS), BF),
            pltpu.VMEM((2 * ROWS, KEYS), BF),
            pltpu.VMEM((ROWS, width), BF),
            pltpu.VMEM((ROWS, width), BF),
            pltpu.VMEM((HEADS, ROWS, HEAD_DIM), BF),
            pltpu.VMEM((HEADS, ROWS, HEAD_DIM), BF),
            pltpu.VMEM((GROUP, 8, ROWS + NOTE, HEAD_DIM), BF),
            pltpu.VMEM((HEADS, RING, ROWS + NOTE, HEAD_DIM), BF),
            pltpu.VMEM((HEADS, ROWS, HEAD_DIM), BF),
            pltpu.VMEM((HEADS, ROWS, HEAD_DIM), BF),
            pltpu.VMEM((ROWS, width), BF),
            pltpu.VMEM((2, ROWS, LATE * HEAD_DIM), BF),
            pltpu.VMEM((4, width, HALF), BF),
            pltpu.VMEM((2, LATE * HEAD_DIM, width), BF),
            pltpu.VMEM((2, ROWS, HALF), BF),
            pltpu.VMEM((2, ROWS, HALF), BF),
            pltpu.VMEM((2, ROWS, HALF), F32),
            pltpu.VMEM((ROWS, width), F32),
            pltpu.VMEM((ROWS, width), BF),
            pltpu.VMEM((ROWS, width), BF),
            pltpu.VMEM((steps, width), F32),
            pltpu.VMEM((ROWS, HEAD_DIM), F32),
            pltpu.VMEM((ROWS, HEAD_DIM), F32),
            dma((KINDS * GROUP,)),
            dma((HEADS, RING)),
            dma((GROUP, 8)),
            dma((GROUP, 4)),
            dma((GROUP, 4)),
            dma((GROUP, 5)),
            dma((GROUP, 5)),
            dma((GROUP, 8)),
            dma((HEADS,)),
            dma((HEADS,)),
            dma((2,)),
            dma((2,)),
            dma((2,)),
            dma((10,)),
            dma((4,)),
            dma((2, LATE)),
            dma((2, LATE)),
        ],
        compiler_params=pltpu.CompilerParams(
            collective_id=0, has_side_effects=True, vmem_limit_bytes=56 * 1024 * 1024
        ),
        cost_estimate=pl.CostEstimate(flops=8_000_000_000, bytes_accessed=12_000_000, transcendentals=12_000_000),
    )(
        fresh_q, fresh_k, fresh_v, stale_k, stale_v, residual, out_weight, gate_table,
        jnp.asarray(frequencies()), positions, timestep,
    )


def solution(mesh):
    in_specs = (
        P("guide", "patch", "tensor"),
        P("guide", "patch", "tensor"),
        P("guide", "patch", "tensor"),
        P("guide", "patch", "tensor"),
        P("guide", "patch", "tensor"),
        P(None, "patch"),
        P("guide", "patch", "tensor"),
        P("tensor", None),
        P(),
        P(),
    )
    out_specs = P("patch", ("tensor", "guide"))
    return jax.shard_map(per_device, mesh=mesh, in_specs=in_specs, out_specs=out_specs, check_vma=False)
```
